32 devices in a mesh: dp: 2 (over x), seq: 16 (over z, y, core).
Axes of the slice: x: 2, y: 2, z: 4, core: 2. Of those that a mesh axis runs over, the one named last changes fastest.
Arguments:
- tokens: bfloat16 [2, 2048, 1280], P('dp', 'seq'), may hold values from -6 to 6
- place: int32 [16, 128], P('seq'), may hold values from 0 to 127, each once within a row
- kernel: float32 [27, 1280], replicated, may hold values from -1.25 to 1.25
- proj_weight: bfloat16 [1280, 3840], P('seq'), may hold values from -0.15625 to 0.15625
- d_projected: bfloat16 [2, 2048, 3840], P('dp', 'seq'), may hold values from -6 to 6
Outputs:
- projected: bfloat16 [2, 2048, 3840], P('dp', 'seq')
- d_tokens: bfloat16 [2, 2048, 1280], P('dp', 'seq')
- d_kernel: float32 [27, 1280], replicated
The draws below stay inside these ranges and needn't reach their ends.
Inputs may be any that keep to these rules, and one draw needn't show every extreme that they name: Each row of place holds every number 0 to 127 once.
All inputs are finite; a program needn't handle non-finite values.
Results may differ from the reference program's by a relative error of at most 0.005.
Values may be sent and summed in bfloat16 or wider, within the bound.
A program may use at most 128 MiB of HBM per device.

```python
import jax
import jax.numpy as jnp
from jax import lax

D = 1280
INLINE = 8
CROSS = 8
TOK_DEV = 128
QKV = 3840
VOLUMES = 2
SEQLEN = 2048
DEPTH = 32
N_SEQ = 16


def block_scale(own_key, extent, split, least, top_value):
    def one(axis_at, shards_of):
        steps = jax.random.uniform(jax.random.fold_in(jax.random.fold_in(own_key, 6), axis_at), (shards_of,), jnp.float32, least / len(split), top_value / len(split))
        return jnp.repeat(jnp.exp(steps), extent[axis_at] // shards_of).reshape((-1,) + (1,) * (len(extent) - axis_at - 1))

    level = one(*split[0])
    for cut in split[1:]:
        level = level * one(*cut)
    return level


def centred(stream_key, extent, scale, most, cuts=(), kind=jnp.bfloat16):
    drawn = jax.random.normal(stream_key, extent, jnp.float32) * scale
    if len(cuts) > 0:
        drawn = block_scale(stream_key, extent, cuts, -0.22, 0.18) * drawn
    return jnp.clip(drawn, min=-most, max=most).astype(kind)


def setup_inputs(seed: int = 0) -> dict:
    arg_keys = jax.random.split(jax.random.key(seed), 6)
    tokens = centred(arg_keys[0], (VOLUMES, SEQLEN, D), 1.0, 6.0, ((0, 2), (1, 16)))
    place = jax.vmap(lambda own: jax.random.permutation(own, TOK_DEV))(jax.random.split(arg_keys[1], N_SEQ)).reshape((N_SEQ, TOK_DEV)).astype(jnp.int32)
    kernel = centred(arg_keys[2], (27, D), 27 ** -0.5, 1.25, (), jnp.float32)
    proj_weight = centred(arg_keys[3], (D, QKV), D ** -0.5, 0.15625, ((0, 16),))
    d_projected = centred(arg_keys[4], (VOLUMES, SEQLEN, QKV), 1.0, 6.0, ((0, 2), (1, 16)))
    return dict(tokens=tokens, place=place, kernel=kernel, proj_weight=proj_weight, d_projected=d_projected)


def grid_index(place):
    group = TOK_DEV // N_SEQ
    scan = jnp.arange(SEQLEN, dtype=jnp.int32)
    device = scan // TOK_DEV
    within = scan % TOK_DEV
    brick = within // group
    slot = device * group + within % group
    return (brick * TOK_DEV + place[brick, slot]).astype(jnp.int32)


def to_grid(rows, target):
    width = rows.shape[-1]
    grid = jnp.zeros((SEQLEN, width), rows.dtype).at[target].set(rows)
    return grid.reshape(DEPTH, INLINE, CROSS, width)


def to_scan(grid, target):
    return grid.reshape(SEQLEN, grid.shape[-1])[target]


def padded(grid):
    return jnp.pad(grid, ((1, 1), (1, 1), (1, 1), (0, 0)))


def window(field, start_z, start_i, start_c):
    return field[start_z:start_z + DEPTH, start_i:start_i + INLINE, start_c:start_c + CROSS].astype(jnp.float32)


def one_volume(tokens, d_projected, target, kernel, proj_weight):
    grid_x = to_grid(tokens, target)
    pad_x = padded(grid_x)
    conv = jnp.zeros(grid_x.shape, jnp.float32)
    for offset in range(27):
        conv = conv + kernel[offset] * window(pad_x, offset // 9, (offset // 3) % 3, offset % 3)
    grid_y = (grid_x.astype(jnp.float32) + conv).astype(jnp.bfloat16)
    rows_y = to_scan(grid_y, target)
    projected = jnp.dot(rows_y, proj_weight, preferred_element_type=jnp.float32).astype(jnp.bfloat16)
    d_y = jnp.dot(d_projected, proj_weight.T, preferred_element_type=jnp.float32).astype(jnp.bfloat16)
    grid_d = to_grid(d_y, target)
    pad_d = padded(grid_d)
    back = grid_d.astype(jnp.float32)
    d_kernel = []
    for offset in range(27):
        dz, di, dc = offset // 9, (offset // 3) % 3, offset % 3
        back = back + kernel[offset] * window(pad_d, 2 - dz, 2 - di, 2 - dc)
        d_kernel.append(jnp.sum(grid_d.astype(jnp.float32) * window(pad_x, dz, di, dc), axis=(0, 1, 2)))
    d_tokens = to_scan(back.astype(jnp.bfloat16), target)
    return projected, d_tokens, jnp.stack(d_kernel)


def reference(tokens, place, kernel, proj_weight, d_projected):
    target = grid_index(place)

    def step(pair):
        return one_volume(pair[0], pair[1], target, kernel, proj_weight)

    projected, d_tokens, d_kernel = lax.map(step, (tokens, d_projected))
    return projected, d_tokens, jnp.sum(d_kernel, axis=0)
```

```python
import functools

import jax
import jax.numpy as jnp
from jax import lax
from jax.experimental import pallas as pl
from jax.experimental.pallas import tpu as pltpu
from jax.sharding import PartitionSpec as P

INLINE = 8
CROSS = 8
MESH = pl.DeviceIdType.MESH
LANES = 128


def with_halo(value, sides, width):
    for axis, dim in sides:
        size, length = (lax.axis_size(axis), value.shape[dim])
        up = [(i, (i + 1) % size) for i in range(size - 1)]
        down = [(j, i) for i, j in up]
        last = lax.slice_in_dim(value, length - width, length, axis=dim)
        first = lax.slice_in_dim(value, 0, width, axis=dim)
        before = lax.ppermute(last, axis, up)
        after = lax.ppermute(first, axis, down)
        value = jnp.concatenate([before, value, after], axis=dim)
    return value


def brick_cells(landed, inverse):
    tokens_dev = inverse.shape[0]
    width = landed.shape[-1]
    slots = landed.reshape(tokens_dev, width)
    cells = jnp.take(slots, inverse, axis=0)
    return cells.reshape(tokens_dev // (INLINE * CROSS), INLINE, CROSS, width)


def scan_pieces(cells, order, count):
    width = cells.shape[-1]
    tokens_dev = order.shape[0]
    slots = jnp.take(cells.reshape(tokens_dev, width), order, axis=0)
    return slots.reshape(count, tokens_dev // count, width)


def to_bricks(rows, inverse, count):
    tokens_dev, width = rows.shape
    landed = lax.all_to_all(
        rows.reshape(count, tokens_dev // count, width),
        "seq",
        split_axis=0,
        concat_axis=0,
        tiled=True,
    )
    return brick_cells(landed, inverse)


def to_scan(cells, order, count):
    landed = lax.all_to_all(
        scan_pieces(cells, order, count), "seq", split_axis=0, concat_axis=0, tiled=True
    )
    return landed.reshape(order.shape[0], cells.shape[-1])


def with_faces(block):
    deeper = with_halo(block, (("seq", 0),), 1)
    return jnp.pad(deeper, ((0, 0), (1, 1), (1, 1), (0, 0)))


def window(field, depth_dev, start_z, start_i, start_c):
    return field[
        start_z : start_z + depth_dev, start_i : start_i + INLINE, start_c : start_c + CROSS
    ].astype(jnp.float32)


def forward_conv(grid_x, pad_x, kernel, depth_dev):
    conv = jnp.zeros(grid_x.shape, jnp.float32)
    for offset in range(27):
        conv = conv + kernel[offset] * window(
            pad_x, depth_dev, offset // 9, offset // 3 % 3, offset % 3
        )
    return (grid_x.astype(jnp.float32) + conv).astype(jnp.bfloat16)


def backward_conv(grid_d, pad_d, pad_x, kernel, depth_dev):
    grid_float = grid_d.astype(jnp.float32)
    back = grid_float
    partial_value = []
    for offset in range(27):
        dz, di, dc = (offset // 9, offset // 3 % 3, offset % 3)
        back = back + kernel[offset] * window(pad_d, depth_dev, 2 - dz, 2 - di, 2 - dc)
        partial_value.append(
            jnp.sum(grid_float * window(pad_x, depth_dev, dz, di, dc), axis=(0, 1, 2))
        )
    return (back.astype(jnp.bfloat16), jnp.stack(partial_value))


def shards(tokens, place, kernel, proj_weight, d_projected):
    count = lax.axis_size("seq")
    order = place[0]
    inverse = jnp.argsort(order)
    rows_x = tokens[0]
    d_rows = d_projected[0]
    depth_dev = rows_x.shape[0] // (INLINE * CROSS)
    d_y = lax.dot_general(
        d_rows,
        lax.all_gather(proj_weight, "seq", axis=0, tiled=True),
        (((1,), (1,)), ((), ())),
        preferred_element_type=jnp.float32,
    )
    d_y = d_y.astype(jnp.bfloat16)
    grid_x = to_bricks(rows_x, inverse, count)
    pad_x = with_faces(grid_x)
    grid_y = forward_conv(grid_x, pad_x, kernel, depth_dev)
    rows_y = to_scan(grid_y, order, count)
    grid_d = to_bricks(d_y, inverse, count)
    pad_d = with_faces(grid_d)
    back, partial_value = backward_conv(grid_d, pad_d, pad_x, kernel, depth_dev)
    d_tokens = to_scan(back, order, count)
    projected = jnp.dot(
        rows_y,
        lax.all_gather(proj_weight, "seq", axis=0, tiled=True),
        preferred_element_type=jnp.float32,
    )
    projected = projected.astype(jnp.bfloat16)
    d_kernel = lax.psum(partial_value, ("dp", "seq"))
    return (projected[None], d_tokens[None], d_kernel)


def fused(
    count,
    tok_ref,
    row_ref,
    col_ref,
    ker_ref,
    w_ref,
    dp_ref,
    proj_ref,
    dtok_ref,
    dker_ref,
    w_all,
    land,
    send,
    edge,
    halo,
    field_x,
    field_d,
    cells,
    sums,
    arrived,
    move_s,
    move_r,
    ring_s,
    ring_r,
    part_s,
    part_r,
    sib_s,
    sib_r,
    halo_s,
    halo_r,
    sum_s,
    sum_r,
):
    me = lax.axis_index("seq")
    plane = lax.axis_index("dp")
    tokens_dev, width = cells.shape
    rows = w_ref.shape[0]
    third = w_ref.shape[1] // 3
    layer = INLINE * CROSS
    depth = tokens_dev // layer
    group = tokens_dev // count
    chips = count // 2
    line = chips // 2
    core = me % 2
    chip = me // 2
    chip_y = chip % 2
    chip_z = chip // 2
    ring = chip_z * (1 - chip_y) + (chips - 1 - chip_z) * chip_y
    sibling = me + 1 - 2 * core
    sign = 1 - 2 * core
    own_third = pl.multiple_of((1 + plane) * third, LANES)
    other_third = pl.multiple_of((2 - plane) * third, LANES)

    def at_ring(position):
        spot = (position + 2 * chips) % chips
        side = spot // line
        z = spot * (1 - side) + (chips - 1 - spot) * side
        return (z * 2 + side) * 2 + core

    def block(shard, start):
        return w_all.at[pl.ds(pl.multiple_of(shard * rows, 16), rows), pl.ds(start, third)]

    def whole(shard):
        return w_all.at[pl.ds(pl.multiple_of(shard * rows, 16), rows), :]

    def remote(src, dst, s_sem, r_sem, target):
        return pltpu.make_async_remote_copy(
            src_ref=src,
            dst_ref=dst,
            send_sem=s_sem,
            recv_sem=r_sem,
            device_id=target,
            device_id_type=MESH,
        )

    edge_zero = jnp.zeros((layer, width), jnp.bfloat16)
    for which in range(2):
        for side in range(2):
            halo[which, side] = edge_zero
    w_all[pl.ds(pl.multiple_of(me * rows, 16), rows), :] = w_ref[...]

    barrier = pltpu.get_barrier_semaphore()
    for step in range(1, count):
        pl.semaphore_signal(
            barrier, inc=1, device_id={"seq": (me + step) % count}, device_id_type=MESH
        )
    pl.semaphore_signal(barrier, inc=1, device_id={"dp": 1 - plane}, device_id_type=MESH)
    pl.semaphore_wait(barrier, count)

    sent = []

    def exchange(which, source):
        copies = []
        for step in range(1, count):
            target = (me + step) % count
            copies.append(
                remote(
                    source.at[target],
                    land.at[which, me],
                    move_s.at[which, step],
                    move_r.at[which, step],
                    {"seq": target},
                )
            )
        for copy in copies:
            copy.start()
        sent.extend(copies)
        land[which, pl.ds(me, 1)] = source[pl.ds(me, 1)]
        return copies

    def landed(which, copies):
        for copy in copies:
            copy.wait_recv()
        value = land[which].astype(jnp.float32)
        return value.reshape(tokens_dev, width).astype(jnp.bfloat16)

    def outgoing(which, slots):
        send[which] = slots.reshape(count, group, width).astype(jnp.bfloat16)
        return exchange(which, send.at[which])

    move_x = exchange(0, tok_ref)

    hops = (line, chips - 1 - line)
    signs = (sign, -sign)

    def ring_copies(way, hop):
        shard = at_ring(ring - signs[way] * (hop - 1))
        target = {"seq": at_ring(ring + signs[way])}
        pair = []
        for piece, start in enumerate((0, own_third)):
            pair.append(
                remote(
                    block(shard, start),
                    block(shard, start),
                    ring_s.at[way, hop, piece],
                    ring_r.at[way, hop, piece],
                    target,
                )
            )
        return pair

    moving = {}
    for way in range(2):
        moving[way, 1] = ring_copies(way, 1)
    for piece in range(2):
        for way in range(2):
            moving[way, 1][piece].start()
    for way in range(2):
        sent.extend(moving[way, 1])
    own_copy = remote(
        whole(me), whole(me), sib_s.at[0, 0, 0], sib_r.at[0, 0, 0], {"seq": sibling}
    )
    own_copy.start()
    sent.append(own_copy)
    to_sibling = [own_copy]
    across = {}

    def sibling_copy(way, hop, piece, shard, start):
        copy = remote(
            block(shard, start),
            block(shard, start),
            sib_s.at[1 + way, hop, piece],
            sib_r.at[1 + way, hop, piece],
            {"seq": sibling},
        )
        copy.start()
        sent.append(copy)
        to_sibling.append(copy)

    def ring_step(hop):
        ways = [way for way in range(2) if hop <= hops[way]]
        for way in ways:
            if hop < hops[way]:
                moving[way, hop + 1] = ring_copies(way, hop + 1)
                sent.extend(moving[way, hop + 1])
        for piece, start in enumerate((0, own_third)):
            for way in ways:
                shard = at_ring(ring - signs[way] * hop)
                moving[way, hop][piece].wait_recv()
                if hop < hops[way]:
                    moving[way, hop + 1][piece].start()
                if piece == 1:
                    copy = remote(
                        block(shard, start),
                        block(shard, start),
                        part_s.at[way, hop],
                        part_r.at[way, hop],
                        {"dp": 1 - plane},
                    )
                    copy.start()
                    sent.append(copy)
                    across[way, hop] = copy
                sibling_copy(way, hop, piece, shard, start)

    def across_step(hop):
        for way in range(2):
            if hop <= hops[way]:
                shard = at_ring(ring - signs[way] * hop)
                across[way, hop].wait_recv()
                sibling_copy(way, hop, 2, shard, other_third)

    square = (tokens_dev, tokens_dev)
    first = lax.broadcasted_iota(jnp.int32, square, 0)
    second = lax.broadcasted_iota(jnp.int32, square, 1)

    def ones_where(mask):
        return jnp.where(mask, 1.0, 0.0).astype(jnp.bfloat16)

    to_cells = ones_where(jnp.broadcast_to(row_ref[...], square) == first)
    to_slots = ones_where(jnp.broadcast_to(col_ref[...], square) == second)
    spot = first % CROSS
    shifts = (
        ones_where((second == first - 1) & (spot > 0)),
        ones_where((second == first + 1) & (spot < CROSS - 1)),
    )

    def times(left, right):
        return jnp.dot(left, right, preferred_element_type=jnp.float32)

    def clear(field):
        pad = jnp.zeros((CROSS, width), jnp.float32)
        for shift in range(3):
            for z in range(depth + 2):
                field[shift, z, 0] = pad
                field[shift, z, INLINE + 1] = pad

    def fill(field, layers, value):
        versions = (times(shifts[0], value), value.astype(jnp.float32), times(shifts[1], value))
        for shift in range(3):
            for at, z in enumerate(layers):
                field[shift, z, pl.ds(1, INLINE)] = versions[shift][
                    at * layer : (at + 1) * layer
                ].reshape(INLINE, CROSS, width)

    def halo_pair(which):
        up = remote(
            edge.at[which, 0],
            halo.at[which, 1],
            halo_s.at[which, 0],
            halo_r.at[which, 0],
            {"seq": (me + count - 1) % count},
        )
        down = remote(
            edge.at[which, 1],
            halo.at[which, 0],
            halo_s.at[which, 1],
            halo_r.at[which, 1],
            {"seq": (me + 1) % count},
        )
        return (up, down)

    def halo_start(which, value):
        edge[which, 0] = value[:layer]
        edge[which, 1] = value[tokens_dev - layer :]
        up, down = halo_pair(which)

        @pl.when(me > 0)
        def _():
            up.start()

        @pl.when(me < count - 1)
        def _():
            down.start()

    def halo_finish(which, field):
        up, down = halo_pair(which)

        @pl.when(me > 0)
        def _():
            down.wait_recv()
            up.wait_send()

        @pl.when(me < count - 1)
        def _():
            up.wait_recv()
            down.wait_send()

        fill(field, (0, depth + 1), halo[which].reshape(2 * layer, width))

    def window(field, z, i, c, lanes):
        return field[c, pl.ds(z, depth), pl.ds(i, INLINE), :, lanes]

    def lanes_of(j):
        return pl.ds(pl.multiple_of(j * LANES, LANES), LANES)

    def convolve(field, flip):
        def body(j, carry):
            lanes = lanes_of(j)
            total = window(field, 1, 1, 1, lanes)
            for offset in range(27):
                z, i, c = (offset // 9, offset // 3 % 3, offset % 3)
                if flip:
                    z, i, c = (2 - z, 2 - i, 2 - c)
                total = total + ker_ref[pl.ds(offset, 1), lanes] * window(field, z, i, c, lanes)
            cells[:, lanes] = total.reshape(tokens_dev, LANES).astype(jnp.bfloat16)
            return carry

        lax.fori_loop(0, width // LANES, body, 0)

    def kernel_sums():
        def body(j, carry):
            lanes = lanes_of(j)
            grad = window(field_d, 1, 1, 1, lanes)
            for offset in range(27):
                z, i, c = (offset // 9, offset // 3 % 3, offset % 3)
                product = grad * window(field_x, z, i, c, lanes)
                sums[0, pl.ds(offset, 1), lanes] = jnp.sum(
                    product.reshape(tokens_dev, LANES), axis=0, keepdims=True
                )
            return carry

        lax.fori_loop(0, width // LANES, body, 0)

    own_layers = tuple(range(1, depth + 1))
    clear(field_x)
    clear(field_d)

    grid_x = times(to_cells, landed(0, move_x)).astype(jnp.bfloat16)
    halo_start(0, grid_x)
    fill(field_x, own_layers, grid_x)
    ring_step(1)
    halo_finish(0, field_x)
    convolve(field_x, False)
    move_y = outgoing(1, times(to_slots, cells[...]))
    for hop in range(2, line + 1):
        ring_step(hop)
        across_step(hop - 1)
    across_step(line)
    for copy in to_sibling:
        copy.wait_recv()

    tile = 2 * LANES

    def back_body(n, carry):
        at = pl.multiple_of(n * tile, tile)
        part = lax.dot_general(
            dp_ref[...],
            w_all[pl.ds(at, tile), :],
            (((1,), (1,)), ((), ())),
            preferred_element_type=jnp.float32,
        )
        send[2, :, :, pl.ds(at, tile)] = part.reshape(count, group, tile).astype(jnp.bfloat16)
        return carry

    lax.fori_loop(0, width // tile, back_body, 0)
    move_d = exchange(2, send.at[2])

    rows_y = landed(1, move_y)

    def front_body(n, carry):
        at = pl.multiple_of(n * tile, tile)
        proj_ref[:, pl.ds(at, tile)] = times(rows_y, w_all[:, pl.ds(at, tile)]).astype(
            jnp.bfloat16
        )
        return carry

    lax.fori_loop(0, w_ref.shape[1] // tile, front_body, 0)

    grid_d = times(to_cells, landed(2, move_d)).astype(jnp.bfloat16)
    halo_start(1, grid_d)
    fill(field_d, own_layers, grid_d)
    kernel_sums()

    partners = [{"seq": sibling}, {"dp": 1 - plane}]
    bit = 2
    while bit < count:
        partners.append({"seq": me + bit - 2 * bit * (me // bit % 2)})
        bit *= 2

    def sum_copy(stage):
        copy = remote(
            sums.at[stage], arrived.at[stage], sum_s.at[stage], sum_r.at[stage], partners[stage]
        )
        copy.start()
        sent.append(copy)
        return copy

    summing = sum_copy(0)
    halo_finish(1, field_d)
    convolve(field_d, True)
    move_b = outgoing(3, times(to_slots, cells[...]))
    for stage in range(len(partners)):
        summing.wait_recv()
        if stage + 1 < len(partners):
            sums[stage + 1] = sums[stage] + arrived[stage]
            summing = sum_copy(stage + 1)
        else:
            dker_ref[...] = sums[stage] + arrived[stage]
    dtok_ref[...] = landed(3, move_b)
    for copy in sent:
        copy.wait_send()


def fused_shards(tokens, place, kernel, proj_weight, d_projected):
    count = lax.axis_size("seq")
    tokens_dev, width = tokens.shape[1:]
    columns = proj_weight.shape[1]
    layer = INLINE * CROSS
    group = tokens_dev // count
    depth = tokens_dev // layer
    stages = count.bit_length()
    line = count // 4
    taps = kernel.shape[0]
    vmem = pl.BlockSpec(memory_space=pltpu.VMEM)
    dma = pltpu.SemaphoreType.DMA
    bf16, f32 = (jnp.bfloat16, jnp.float32)
    projected, d_tokens, d_kernel = pl.pallas_call(
        functools.partial(fused, count),
        out_shape=(
            jax.ShapeDtypeStruct((tokens_dev, columns), bf16),
            jax.ShapeDtypeStruct((tokens_dev, width), bf16),
            jax.ShapeDtypeStruct((taps, width), f32),
        ),
        in_specs=[vmem] * 6,
        out_specs=(vmem, vmem, vmem),
        scratch_shapes=[
            pltpu.VMEM((width, columns), bf16),
            pltpu.VMEM((4, count, group, width), bf16),
            pltpu.VMEM((4, count, group, width), bf16),
            pltpu.VMEM((2, 2, layer, width), bf16),
            pltpu.VMEM((2, 2, layer, width), bf16),
            pltpu.VMEM((3, depth + 2, INLINE + 2, CROSS, width), f32),
            pltpu.VMEM((3, depth + 2, INLINE + 2, CROSS, width), f32),
            pltpu.VMEM((tokens_dev, width), bf16),
            pltpu.VMEM((stages, taps, width), f32),
            pltpu.VMEM((stages, taps, width), f32),
            dma((4, count)),
            dma((4, count)),
            dma((2, line + 1, 2)),
            dma((2, line + 1, 2)),
            dma((2, line + 1)),
            dma((2, line + 1)),
            dma((3, line + 1, 3)),
            dma((3, line + 1, 3)),
            dma((2, 2)),
            dma((2, 2)),
            dma((stages,)),
            dma((stages,)),
        ],
        compiler_params=pltpu.CompilerParams(
            collective_id=0, has_side_effects=True, vmem_limit_bytes=56 * 1024 * 1024
        ),
        cost_estimate=pl.CostEstimate(
            flops=4 * tokens_dev * width * columns,
            bytes_accessed=4 * tokens_dev * columns,
            transcendentals=0,
        ),
    )(
        tokens[0].reshape(count, group, width),
        place,
        place.reshape(tokens_dev, 1),
        kernel,
        proj_weight,
        d_projected[0],
    )
    return (projected[None], d_tokens[None], d_kernel)


def solution(mesh):
    placed = (P("dp", "seq", None), P("seq", None), P(), P("seq", None), P("dp", "seq", None))
    count = mesh.shape["seq"]
    use_kernel = mesh.shape["dp"] == 2 and count == 16
    return jax.shard_map(
        fused_shards if use_kernel else shards,
        mesh=mesh,
        in_specs=placed,
        out_specs=(P("dp", "seq", None), P("dp", "seq", None), P()),
        check_vma=False,
    )
```

```python
import functools

import jax
import jax.numpy as jnp
from jax import lax
from jax.experimental import pallas as pl
from jax.experimental.pallas import tpu as pltpu
from jax.sharding import PartitionSpec as P

INLINE = 8
CROSS = 8
MESH = pl.DeviceIdType.MESH
LANES = 128


def with_halo(value, sides, width):
    for axis, dim in sides:
        size, length = (lax.axis_size(axis), value.shape[dim])
        up = [(i, (i + 1) % size) for i in range(size - 1)]
        down = [(j, i) for i, j in up]
        last = lax.slice_in_dim(value, length - width, length, axis=dim)
        first = lax.slice_in_dim(value, 0, width, axis=dim)
        before = lax.ppermute(last, axis, up)
        after = lax.ppermute(first, axis, down)
        value = jnp.concatenate([before, value, after], axis=dim)
    return value


def brick_cells(landed, inverse):
    tokens_dev = inverse.shape[0]
    width = landed.shape[-1]
    slots = landed.reshape(tokens_dev, width)
    cells = jnp.take(slots, inverse, axis=0)
    return cells.reshape(tokens_dev // (INLINE * CROSS), INLINE, CROSS, width)


def scan_pieces(cells, order, count):
    width = cells.shape[-1]
    tokens_dev = order.shape[0]
    slots = jnp.take(cells.reshape(tokens_dev, width), order, axis=0)
    return slots.reshape(count, tokens_dev // count, width)


def to_bricks(rows, inverse, count):
    tokens_dev, width = rows.shape
    landed = lax.all_to_all(
        rows.reshape(count, tokens_dev // count, width),
        "seq",
        split_axis=0,
        concat_axis=0,
        tiled=True,
    )
    return brick_cells(landed, inverse)


def to_scan(cells, order, count):
    landed = lax.all_to_all(
        scan_pieces(cells, order, count), "seq", split_axis=0, concat_axis=0, tiled=True
    )
    return landed.reshape(order.shape[0], cells.shape[-1])


def with_faces(block):
    deeper = with_halo(block, (("seq", 0),), 1)
    return jnp.pad(deeper, ((0, 0), (1, 1), (1, 1), (0, 0)))


def window(field, depth_dev, start_z, start_i, start_c):
    return field[
        start_z : start_z + depth_dev, start_i : start_i + INLINE, start_c : start_c + CROSS
    ].astype(jnp.float32)


def forward_conv(grid_x, pad_x, kernel, depth_dev):
    conv = jnp.zeros(grid_x.shape, jnp.float32)
    for offset in range(27):
        conv = conv + kernel[offset] * window(
            pad_x, depth_dev, offset // 9, offset // 3 % 3, offset % 3
        )
    return (grid_x.astype(jnp.float32) + conv).astype(jnp.bfloat16)


def backward_conv(grid_d, pad_d, pad_x, kernel, depth_dev):
    grid_float = grid_d.astype(jnp.float32)
    back = grid_float
    partial_value = []
    for offset in range(27):
        dz, di, dc = (offset // 9, offset // 3 % 3, offset % 3)
        back = back + kernel[offset] * window(pad_d, depth_dev, 2 - dz, 2 - di, 2 - dc)
        partial_value.append(
            jnp.sum(grid_float * window(pad_x, depth_dev, dz, di, dc), axis=(0, 1, 2))
        )
    return (back.astype(jnp.bfloat16), jnp.stack(partial_value))


def shards(tokens, place, kernel, proj_weight, d_projected):
    count = lax.axis_size("seq")
    order = place[0]
    inverse = jnp.argsort(order)
    rows_x = tokens[0]
    d_rows = d_projected[0]
    depth_dev = rows_x.shape[0] // (INLINE * CROSS)
    d_y = lax.dot_general(
        d_rows,
        lax.all_gather(proj_weight, "seq", axis=0, tiled=True),
        (((1,), (1,)), ((), ())),
        preferred_element_type=jnp.float32,
    )
    d_y = d_y.astype(jnp.bfloat16)
    grid_x = to_bricks(rows_x, inverse, count)
    pad_x = with_faces(grid_x)
    grid_y = forward_conv(grid_x, pad_x, kernel, depth_dev)
    rows_y = to_scan(grid_y, order, count)
    grid_d = to_bricks(d_y, inverse, count)
    pad_d = with_faces(grid_d)
    back, partial_value = backward_conv(grid_d, pad_d, pad_x, kernel, depth_dev)
    d_tokens = to_scan(back, order, count)
    projected = jnp.dot(
        rows_y,
        lax.all_gather(proj_weight, "seq", axis=0, tiled=True),
        preferred_element_type=jnp.float32,
    )
    projected = projected.astype(jnp.bfloat16)
    d_kernel = lax.psum(partial_value, ("dp", "seq"))
    return (projected[None], d_tokens[None], d_kernel)


def fused(
    count,
    tok_ref,
    row_ref,
    ker_ref,
    w_ref,
    dp_ref,
    proj_ref,
    dtok_ref,
    dker_ref,
    w_all,
    land,
    send,
    edge,
    halo,
    field_x,
    field_d,
    cells,
    turned,
    back_rows,
    sums,
    arrived,
    move_s,
    move_r,
    ring_s,
    ring_r,
    part_s,
    part_r,
    sib_s,
    sib_r,
    halo_s,
    halo_r,
    sum_s,
    sum_r,
):
    me = lax.axis_index("seq")
    plane = lax.axis_index("dp")
    tokens_dev, width = cells.shape
    rows = w_ref.shape[0]
    third = w_ref.shape[1] // 3
    layer = INLINE * CROSS
    depth = tokens_dev // layer
    group = tokens_dev // count
    chips = count // 2
    line = chips // 2
    core = me % 2
    chip = me // 2
    chip_y = chip % 2
    chip_z = chip // 2
    ring = chip_z * (1 - chip_y) + (chips - 1 - chip_z) * chip_y
    sibling = me + 1 - 2 * core
    sign = 1 - 2 * core
    own_third = pl.multiple_of((1 + plane) * third, LANES)
    other_third = pl.multiple_of((2 - plane) * third, LANES)

    def at_ring(position):
        spot = (position + 2 * chips) % chips
        side = spot // line
        z = spot * (1 - side) + (chips - 1 - spot) * side
        return (z * 2 + side) * 2 + core

    def block(shard, start):
        return w_all.at[pl.ds(pl.multiple_of(shard * rows, 16), rows), pl.ds(start, third)]

    def whole(shard):
        return w_all.at[pl.ds(pl.multiple_of(shard * rows, 16), rows), :]

    def remote(src, dst, s_sem, r_sem, target):
        return pltpu.make_async_remote_copy(
            src_ref=src,
            dst_ref=dst,
            send_sem=s_sem,
            recv_sem=r_sem,
            device_id=target,
            device_id_type=MESH,
        )

    edge_zero = jnp.zeros((layer, width), jnp.bfloat16)
    for which in range(2):
        for side in range(2):
            halo[which, side] = edge_zero
    w_all[pl.ds(pl.multiple_of(me * rows, 16), rows), :] = w_ref[...]

    barrier = pltpu.get_barrier_semaphore()
    for step in range(1, count):
        pl.semaphore_signal(
            barrier, inc=1, device_id={"seq": (me + step) % count}, device_id_type=MESH
        )
    pl.semaphore_signal(barrier, inc=1, device_id={"dp": 1 - plane}, device_id_type=MESH)
    pl.semaphore_wait(barrier, count)

    sent = []

    def exchange(which, source):
        copies = []
        for step in range(1, count):
            target = (me + step) % count
            copies.append(
                remote(
                    source.at[target],
                    land.at[which, me],
                    move_s.at[which, step],
                    move_r.at[which, step],
                    {"seq": target},
                )
            )
        for copy in copies:
            copy.start()
        sent.extend(copies)
        land[which, pl.ds(me, 1)] = source[pl.ds(me, 1)]
        return copies

    def landed(which, copies):
        for copy in copies:
            copy.wait_recv()
        value = land[which].astype(jnp.float32)
        return value.reshape(tokens_dev, width).astype(jnp.bfloat16)

    def outgoing(which, slots):
        send[which] = slots.reshape(count, group, width).astype(jnp.bfloat16)
        return exchange(which, send.at[which])

    move_x = exchange(0, tok_ref)

    hops = (line, chips - 1 - line)
    signs = (sign, -sign)

    def ring_copies(way, hop):
        shard = at_ring(ring - signs[way] * (hop - 1))
        target = {"seq": at_ring(ring + signs[way])}
        pair = []
        for piece, start in enumerate((0, own_third)):
            pair.append(
                remote(
                    block(shard, start),
                    block(shard, start),
                    ring_s.at[way, hop, piece],
                    ring_r.at[way, hop, piece],
                    target,
                )
            )
        return pair

    moving = {}
    for way in range(2):
        moving[way, 1] = ring_copies(way, 1)
    for piece in (1, 0):
        for way in range(2):
            moving[way, 1][piece].start()
    for way in range(2):
        sent.extend(moving[way, 1])
    own_copy = remote(
        whole(me), whole(me), sib_s.at[0, 0, 0], sib_r.at[0, 0, 0], {"seq": sibling}
    )
    own_copy.start()
    sent.append(own_copy)
    to_sibling = {(0, 0): [own_copy]}
    across = {}

    def sibling_copy(way, hop, piece, shard, start):
        copy = remote(
            block(shard, start),
            block(shard, start),
            sib_s.at[1 + way, hop, piece],
            sib_r.at[1 + way, hop, piece],
            {"seq": sibling},
        )
        copy.start()
        sent.append(copy)
        to_sibling.setdefault((way, hop), []).append(copy)

    def ring_step(hop):
        ways = [way for way in range(2) if hop <= hops[way]]
        for way in ways:
            if hop < hops[way]:
                moving[way, hop + 1] = ring_copies(way, hop + 1)
                sent.extend(moving[way, hop + 1])
        for piece, start in ((1, own_third), (0, 0)):
            for way in ways:
                shard = at_ring(ring - signs[way] * hop)
                moving[way, hop][piece].wait_recv()
                if hop < hops[way]:
                    moving[way, hop + 1][piece].start()
                if piece == 1:
                    copy = remote(
                        block(shard, start),
                        block(shard, start),
                        part_s.at[way, hop],
                        part_r.at[way, hop],
                        {"dp": 1 - plane},
                    )
                    copy.start()
                    sent.append(copy)
                    across[way, hop] = copy
                sibling_copy(way, hop, piece, shard, start)

    def across_step(hop):
        for way in range(2):
            if hop <= hops[way]:
                shard = at_ring(ring - signs[way] * hop)
                across[way, hop].wait_recv()
                sibling_copy(way, hop, 2, shard, other_third)

    square = (tokens_dev, tokens_dev)
    first = lax.broadcasted_iota(jnp.int32, square, 0)
    second = lax.broadcasted_iota(jnp.int32, square, 1)

    def ones_where(mask):
        return jnp.where(mask, 1.0, 0.0).astype(jnp.bfloat16)

    chosen = jnp.where(jnp.broadcast_to(row_ref[...], square) == first, 1.0, 0.0)
    to_cells = chosen.astype(jnp.bfloat16)
    to_slots = chosen.T.astype(jnp.bfloat16)
    same = ones_where(first == second)
    spot = first % CROSS
    shifts = (
        ones_where((second == first - 1) & (spot > 0)),
        ones_where((second == first + 1) & (spot < CROSS - 1)),
    )

    def times(left, right):
        return jnp.dot(left, right, preferred_element_type=jnp.float32)

    def clear(field):
        pad = jnp.zeros((CROSS, width), jnp.float32)
        for shift in range(3):
            for z in range(depth + 2):
                field[shift, z, 0] = pad
                field[shift, z, INLINE + 1] = pad

    def fill(field, layers, value):
        versions = (times(shifts[0], value), value.astype(jnp.float32), times(shifts[1], value))
        for shift in range(3):
            for at, z in enumerate(layers):
                field[shift, z, pl.ds(1, INLINE)] = versions[shift][
                    at * layer : (at + 1) * layer
                ].reshape(INLINE, CROSS, width)

    def halo_pair(which):
        up = remote(
            edge.at[which, 0],
            halo.at[which, 1],
            halo_s.at[which, 0],
            halo_r.at[which, 0],
            {"seq": (me + count - 1) % count},
        )
        down = remote(
            edge.at[which, 1],
            halo.at[which, 0],
            halo_s.at[which, 1],
            halo_r.at[which, 1],
            {"seq": (me + 1) % count},
        )
        return (up, down)

    def halo_start(which, value):
        edge[which, 0] = value[:layer]
        edge[which, 1] = value[tokens_dev - layer :]
        up, down = halo_pair(which)

        @pl.when(me > 0)
        def _():
            up.start()

        @pl.when(me < count - 1)
        def _():
            down.start()

    def halo_finish(which, field):
        up, down = halo_pair(which)

        @pl.when(me > 0)
        def _():
            down.wait_recv()
            up.wait_send()

        @pl.when(me < count - 1)
        def _():
            up.wait_recv()
            down.wait_send()

        fill(field, (0, depth + 1), halo[which].reshape(2 * layer, width))

    def window(field, z, i, c, lanes):
        return field[c, pl.ds(z, depth), pl.ds(i, INLINE), :, lanes]

    def lanes_of(j):
        return pl.ds(pl.multiple_of(j * LANES, LANES), LANES)

    def convolve(field, flip, start, stop):
        def body(j, carry):
            lanes = lanes_of(j)
            total = window(field, 1, 1, 1, lanes)
            for offset in range(27):
                z, i, c = (offset // 9, offset // 3 % 3, offset % 3)
                if flip:
                    z, i, c = (2 - z, 2 - i, 2 - c)
                total = total + ker_ref[pl.ds(offset, 1), lanes] * window(field, z, i, c, lanes)
            cells[:, lanes] = total.reshape(tokens_dev, LANES).astype(jnp.bfloat16)
            return carry

        lax.fori_loop(start, stop, body, 0)

    def kernel_sums():
        def body(j, carry):
            lanes = lanes_of(j)
            grad = window(field_d, 1, 1, 1, lanes)
            for offset in range(27):
                z, i, c = (offset // 9, offset // 3 % 3, offset % 3)
                product = grad * window(field_x, z, i, c, lanes)
                sums[0, pl.ds(offset, 1), lanes] = jnp.sum(
                    product.reshape(tokens_dev, LANES), axis=0, keepdims=True
                )
            return carry

        lax.fori_loop(0, width // LANES, body, 0)

    tile = 2 * LANES
    chunks = width // LANES
    own_layers = tuple(range(1, depth + 1))

    def turn_body(n, carry):
        at = pl.multiple_of(n * LANES, LANES)
        turned[pl.ds(at, LANES), :] = (
            dp_ref[:, pl.ds(at, LANES)].astype(jnp.float32).T.astype(jnp.bfloat16)
        )
        return carry

    def back_chip(position):
        at = pl.ds(pl.multiple_of(at_ring(position) // 2 * (2 * rows), 16), 2 * rows)
        back_rows[at, :] = times(w_all[at, :], turned[...]).astype(jnp.bfloat16)

    def back_step(hop):
        for way in range(2):
            for copy in to_sibling.get((way, hop), ()):
                copy.wait_recv()
        if hop <= min(hops):
            back_chip(ring - hop)
        if hop > 0:
            back_chip(ring + hop)

    lax.fori_loop(0, w_ref.shape[1] // LANES, turn_body, 0)
    clear(field_x)
    clear(field_d)
    ring_step(1)
    grid_x = times(to_cells, landed(0, move_x)).astype(jnp.bfloat16)
    halo_start(0, grid_x)
    fill(field_x, own_layers, grid_x)
    across_step(1)
    back_step(0)
    ring_step(2)
    halo_finish(0, field_x)
    back_step(1)
    across_step(2)
    for hop in range(3, line + 1):
        ring_step(hop)
        back_step(hop - 1)
        across_step(hop)
    back_step(line)

    move_d = outgoing(
        2,
        lax.dot_general(
            same,
            back_rows[...],
            (((1,), (1,)), ((), ())),
            preferred_element_type=jnp.float32,
        ),
    )
    convolve(field_x, False, 0, chunks)
    move_y = outgoing(1, times(to_slots, cells[...]))

    grid_d = times(to_cells, landed(2, move_d)).astype(jnp.bfloat16)
    halo_start(1, grid_d)
    fill(field_d, own_layers, grid_d)
    kernel_sums()

    partners = [{"seq": sibling}, {"dp": 1 - plane}]
    bit = 2
    while bit < count:
        partners.append({"seq": me + bit - 2 * bit * (me // bit % 2)})
        bit *= 2
    stages = len(partners)

    def sum_copy(stage):
        copy = remote(
            sums.at[stage], arrived.at[stage], sum_s.at[stage], sum_r.at[stage], partners[stage]
        )
        copy.start()
        sent.append(copy)
        return copy

    def sum_step(stage, copy):
        copy.wait_recv()
        if stage + 1 == stages:
            dker_ref[...] = sums[stage] + arrived[stage]
            return copy
        sums[stage + 1] = sums[stage] + arrived[stage]
        return sum_copy(stage + 1)

    summing = sum_copy(0)
    halo_finish(1, field_d)
    convolve(field_d, True, 0, chunks // 2)
    summing = sum_step(0, summing)
    convolve(field_d, True, chunks // 2, chunks)
    move_b = outgoing(3, times(to_slots, cells[...]))
    summing = sum_step(1, summing)

    rows_y = landed(1, move_y)
    tiles = w_ref.shape[1] // tile

    def front_body(n, carry):
        at = pl.multiple_of(n * tile, tile)
        proj_ref[:, pl.ds(at, tile)] = times(rows_y, w_all[:, pl.ds(at, tile)]).astype(
            jnp.bfloat16
        )
        return carry

    for stage in range(2, stages):
        part = (stage - 2, stage - 1)
        low, high = [tiles * p // (stages - 2) for p in part]
        lax.fori_loop(low, high, front_body, 0)
        summing = sum_step(stage, summing)
    dtok_ref[...] = landed(3, move_b)
    for copy in sent:
        copy.wait_send()


def fused_shards(tokens, place, kernel, proj_weight, d_projected):
    count = lax.axis_size("seq")
    tokens_dev, width = tokens.shape[1:]
    columns = proj_weight.shape[1]
    layer = INLINE * CROSS
    group = tokens_dev // count
    depth = tokens_dev // layer
    stages = count.bit_length()
    line = count // 4
    taps = kernel.shape[0]
    vmem = pl.BlockSpec(memory_space=pltpu.VMEM)
    dma = pltpu.SemaphoreType.DMA
    bf16, f32 = (jnp.bfloat16, jnp.float32)
    projected, d_tokens, d_kernel = pl.pallas_call(
        functools.partial(fused, count),
        out_shape=(
            jax.ShapeDtypeStruct((tokens_dev, columns), bf16),
            jax.ShapeDtypeStruct((tokens_dev, width), bf16),
            jax.ShapeDtypeStruct((taps, width), f32),
        ),
        in_specs=[vmem] * 5,
        out_specs=(vmem, vmem, vmem),
        scratch_shapes=[
            pltpu.VMEM((width, columns), bf16),
            pltpu.VMEM((4, count, group, width), bf16),
            pltpu.VMEM((4, count, group, width), bf16),
            pltpu.VMEM((2, 2, layer, width), bf16),
            pltpu.VMEM((2, 2, layer, width), bf16),
            pltpu.VMEM((3, depth + 2, INLINE + 2, CROSS, width), f32),
            pltpu.VMEM((3, depth + 2, INLINE + 2, CROSS, width), f32),
            pltpu.VMEM((tokens_dev, width), bf16),
            pltpu.VMEM((columns, tokens_dev), bf16),
            pltpu.VMEM((width, tokens_dev), bf16),
            pltpu.VMEM((stages, taps, width), f32),
            pltpu.VMEM((stages, taps, width), f32),
            dma((4, count)),
            dma((4, count)),
            dma((2, line + 1, 2)),
            dma((2, line + 1, 2)),
            dma((2, line + 1)),
            dma((2, line + 1)),
            dma((3, line + 1, 3)),
            dma((3, line + 1, 3)),
            dma((2, 2)),
            dma((2, 2)),
            dma((stages,)),
            dma((stages,)),
        ],
        compiler_params=pltpu.CompilerParams(
            collective_id=0, has_side_effects=True, vmem_limit_bytes=56 * 1024 * 1024
        ),
        cost_estimate=pl.CostEstimate(
            flops=4 * tokens_dev * width * columns,
            bytes_accessed=4 * tokens_dev * columns,
            transcendentals=0,
        ),
    )(
        tokens[0].reshape(count, group, width),
        place,
        kernel,
        proj_weight,
        d_projected[0],
    )
    return (projected[None], d_tokens[None], d_kernel)


def solution(mesh):
    placed = (P("dp", "seq", None), P("seq", None), P(), P("seq", None), P("dp", "seq", None))
    count = mesh.shape["seq"]
    use_kernel = mesh.shape["dp"] == 2 and count == 16
    return jax.shard_map(
        fused_shards if use_kernel else shards,
        mesh=mesh,
        in_specs=placed,
        out_specs=(P("dp", "seq", None), P("dp", "seq", None), P()),
        check_vma=False,
    )
```

```python
import functools

import jax
import jax.numpy as jnp
from jax import lax
from jax.experimental import pallas as pl
from jax.experimental.pallas import tpu as pltpu
from jax.sharding import PartitionSpec as P

INLINE = 8
CROSS = 8
MESH = pl.DeviceIdType.MESH
LANES = 128


def with_halo(value, sides, width):
    for axis, dim in sides:
        size, length = (lax.axis_size(axis), value.shape[dim])
        up = [(i, (i + 1) % size) for i in range(size - 1)]
        down = [(j, i) for i, j in up]
        last = lax.slice_in_dim(value, length - width, length, axis=dim)
        first = lax.slice_in_dim(value, 0, width, axis=dim)
        before = lax.ppermute(last, axis, up)
        after = lax.ppermute(first, axis, down)
        value = jnp.concatenate([before, value, after], axis=dim)
    return value


def brick_cells(landed, inverse):
    tokens_dev = inverse.shape[0]
    width = landed.shape[-1]
    slots = landed.reshape(tokens_dev, width)
    cells = jnp.take(slots, inverse, axis=0)
    return cells.reshape(tokens_dev // (INLINE * CROSS), INLINE, CROSS, width)


def scan_pieces(cells, order, count):
    width = cells.shape[-1]
    tokens_dev = order.shape[0]
    slots = jnp.take(cells.reshape(tokens_dev, width), order, axis=0)
    return slots.reshape(count, tokens_dev // count, width)


def to_bricks(rows, inverse, count):
    tokens_dev, width = rows.shape
    landed = lax.all_to_all(
        rows.reshape(count, tokens_dev // count, width),
        "seq",
        split_axis=0,
        concat_axis=0,
        tiled=True,
    )
    return brick_cells(landed, inverse)


def to_scan(cells, order, count):
    landed = lax.all_to_all(
        scan_pieces(cells, order, count), "seq", split_axis=0, concat_axis=0, tiled=True
    )
    return landed.reshape(order.shape[0], cells.shape[-1])


def with_faces(block):
    deeper = with_halo(block, (("seq", 0),), 1)
    return jnp.pad(deeper, ((0, 0), (1, 1), (1, 1), (0, 0)))


def window(field, depth_dev, start_z, start_i, start_c):
    return field[
        start_z : start_z + depth_dev, start_i : start_i + INLINE, start_c : start_c + CROSS
    ].astype(jnp.float32)


def forward_conv(grid_x, pad_x, kernel, depth_dev):
    conv = jnp.zeros(grid_x.shape, jnp.float32)
    for offset in range(27):
        conv = conv + kernel[offset] * window(
            pad_x, depth_dev, offset // 9, offset // 3 % 3, offset % 3
        )
    return (grid_x.astype(jnp.float32) + conv).astype(jnp.bfloat16)


def backward_conv(grid_d, pad_d, pad_x, kernel, depth_dev):
    grid_float = grid_d.astype(jnp.float32)
    back = grid_float
    partial_value = []
    for offset in range(27):
        dz, di, dc = (offset // 9, offset // 3 % 3, offset % 3)
        back = back + kernel[offset] * window(pad_d, depth_dev, 2 - dz, 2 - di, 2 - dc)
        partial_value.append(
            jnp.sum(grid_float * window(pad_x, depth_dev, dz, di, dc), axis=(0, 1, 2))
        )
    return (back.astype(jnp.bfloat16), jnp.stack(partial_value))


def shards(tokens, place, kernel, proj_weight, d_projected):
    count = lax.axis_size("seq")
    order = place[0]
    inverse = jnp.argsort(order)
    rows_x = tokens[0]
    d_rows = d_projected[0]
    depth_dev = rows_x.shape[0] // (INLINE * CROSS)
    d_y = lax.dot_general(
        d_rows,
        lax.all_gather(proj_weight, "seq", axis=0, tiled=True),
        (((1,), (1,)), ((), ())),
        preferred_element_type=jnp.float32,
    )
    d_y = d_y.astype(jnp.bfloat16)
    grid_x = to_bricks(rows_x, inverse, count)
    pad_x = with_faces(grid_x)
    grid_y = forward_conv(grid_x, pad_x, kernel, depth_dev)
    rows_y = to_scan(grid_y, order, count)
    grid_d = to_bricks(d_y, inverse, count)
    pad_d = with_faces(grid_d)
    back, partial_value = backward_conv(grid_d, pad_d, pad_x, kernel, depth_dev)
    d_tokens = to_scan(back, order, count)
    projected = jnp.dot(
        rows_y,
        lax.all_gather(proj_weight, "seq", axis=0, tiled=True),
        preferred_element_type=jnp.float32,
    )
    projected = projected.astype(jnp.bfloat16)
    d_kernel = lax.psum(partial_value, ("dp", "seq"))
    return (projected[None], d_tokens[None], d_kernel)


def fused(
    count,
    tok_ref,
    row_ref,
    ker_ref,
    w_ref,
    dp_ref,
    proj_ref,
    dtok_ref,
    dker_ref,
    w_all,
    land,
    send,
    edge,
    halo,
    field_x,
    field_d,
    cells,
    turned,
    back_rows,
    sums,
    arrived,
    total,
    move_s,
    move_r,
    ring_s,
    ring_r,
    part_s,
    part_r,
    sib_s,
    sib_r,
    halo_s,
    halo_r,
    sum_s,
    sum_r,
):
    me = lax.axis_index("seq")
    plane = lax.axis_index("dp")
    tokens_dev, width = cells.shape
    rows = w_ref.shape[0]
    third = w_ref.shape[1] // 3
    layer = INLINE * CROSS
    depth = tokens_dev // layer
    group = tokens_dev // count
    chips = count // 2
    line = chips // 2
    core = me % 2
    chip = me // 2
    chip_y = chip % 2
    chip_z = chip // 2
    ring = chip_z * (1 - chip_y) + (chips - 1 - chip_z) * chip_y
    sibling = me + 1 - 2 * core
    sign = 1 - 2 * core
    own_third = pl.multiple_of((1 + plane) * third, LANES)
    other_third = pl.multiple_of((2 - plane) * third, LANES)

    def at_ring(position):
        spot = (position + 2 * chips) % chips
        side = spot // line
        z = spot * (1 - side) + (chips - 1 - spot) * side
        return (z * 2 + side) * 2 + core

    def block(shard, start):
        return w_all.at[pl.ds(pl.multiple_of(shard * rows, 16), rows), pl.ds(start, third)]

    def whole(shard):
        return w_all.at[pl.ds(pl.multiple_of(shard * rows, 16), rows), :]

    def remote(src, dst, s_sem, r_sem, target):
        return pltpu.make_async_remote_copy(
            src_ref=src,
            dst_ref=dst,
            send_sem=s_sem,
            recv_sem=r_sem,
            device_id=target,
            device_id_type=MESH,
        )

    edge_zero = jnp.zeros((layer, width), jnp.bfloat16)
    for which in range(2):
        for side in range(2):
            halo[which, side] = edge_zero
    w_all[pl.ds(pl.multiple_of(me * rows, 16), rows), :] = w_ref[...]

    barrier = pltpu.get_barrier_semaphore()
    for step in range(1, count):
        pl.semaphore_signal(
            barrier, inc=1, device_id={"seq": (me + step) % count}, device_id_type=MESH
        )
    pl.semaphore_signal(barrier, inc=1, device_id={"dp": 1 - plane}, device_id_type=MESH)
    pl.semaphore_wait(barrier, count)

    sent = []

    def exchange(which, source):
        copies = []
        for step in range(1, count):
            target = (me + step) % count
            copies.append(
                remote(
                    source.at[target],
                    land.at[which, me],
                    move_s.at[which, step],
                    move_r.at[which, step],
                    {"seq": target},
                )
            )
        for copy in copies:
            copy.start()
        sent.extend(copies)
        land[which, pl.ds(me, 1)] = source[pl.ds(me, 1)]
        return copies

    def landed(which, copies):
        for copy in copies:
            copy.wait_recv()
        value = land[which].astype(jnp.float32)
        return value.reshape(tokens_dev, width).astype(jnp.bfloat16)

    def outgoing(which, slots):
        send[which] = slots.reshape(count, group, width).astype(jnp.bfloat16)
        return exchange(which, send.at[which])

    hops = (line, chips - 1 - line)
    signs = (sign, -sign)

    def ring_copies(way, hop):
        shard = at_ring(ring - signs[way] * (hop - 1))
        target = {"seq": at_ring(ring + signs[way])}
        pair = []
        for piece, start in enumerate((0, own_third)):
            pair.append(
                remote(
                    block(shard, start),
                    block(shard, start),
                    ring_s.at[way, hop, piece],
                    ring_r.at[way, hop, piece],
                    target,
                )
            )
        return pair

    moving = {}
    for way in range(2):
        moving[way, 1] = ring_copies(way, 1)
    for piece in (1, 0):
        for way in range(2):
            moving[way, 1][piece].start()
    for way in range(2):
        sent.extend(moving[way, 1])
    own_copy = remote(
        whole(me), whole(me), sib_s.at[0, 0, 0], sib_r.at[0, 0, 0], {"seq": sibling}
    )
    own_copy.start()
    sent.append(own_copy)
    to_sibling = {(0, 0): [own_copy]}
    across = {}

    def sibling_copy(way, hop, piece, shard, start):
        copy = remote(
            block(shard, start),
            block(shard, start),
            sib_s.at[1 + way, hop, piece],
            sib_r.at[1 + way, hop, piece],
            {"seq": sibling},
        )
        copy.start()
        sent.append(copy)
        to_sibling.setdefault((way, hop), []).append(copy)

    def ring_step(hop):
        ways = [way for way in range(2) if hop <= hops[way]]
        for way in ways:
            if hop < hops[way]:
                moving[way, hop + 1] = ring_copies(way, hop + 1)
                sent.extend(moving[way, hop + 1])
        for piece, start in ((1, own_third), (0, 0)):
            for way in ways:
                shard = at_ring(ring - signs[way] * hop)
                moving[way, hop][piece].wait_recv()
                if hop < hops[way]:
                    moving[way, hop + 1][piece].start()
                if piece == 1:
                    copy = remote(
                        block(shard, start),
                        block(shard, start),
                        part_s.at[way, hop],
                        part_r.at[way, hop],
                        {"dp": 1 - plane},
                    )
                    copy.start()
                    sent.append(copy)
                    across[way, hop] = copy
                sibling_copy(way, hop, piece, shard, start)

    def across_step(hop):
        for way in range(2):
            if hop <= hops[way]:
                shard = at_ring(ring - signs[way] * hop)
                across[way, hop].wait_recv()
                sibling_copy(way, hop, 2, shard, other_third)

    square = (tokens_dev, tokens_dev)
    first = lax.broadcasted_iota(jnp.int32, square, 0)
    second = lax.broadcasted_iota(jnp.int32, square, 1)

    def ones_where(mask):
        return jnp.where(mask, 1.0, 0.0).astype(jnp.bfloat16)

    chosen = jnp.where(jnp.broadcast_to(row_ref[...], square) == first, 1.0, 0.0)
    to_cells = chosen.astype(jnp.bfloat16)
    to_slots = chosen.T.astype(jnp.bfloat16)
    same = ones_where(first == second)
    spot = first % CROSS
    shifts = (
        ones_where((second == first - 1) & (spot > 0)),
        ones_where((second == first + 1) & (spot < CROSS - 1)),
    )

    def times(left, right):
        return jnp.dot(left, right, preferred_element_type=jnp.float32)

    def clear(field):
        pad = jnp.zeros((CROSS, width), jnp.float32)
        for shift in range(3):
            for z in range(depth + 2):
                field[shift, z, 0] = pad
                field[shift, z, INLINE + 1] = pad

    def fill(field, layers, value):
        versions = (times(shifts[0], value), value.astype(jnp.float32), times(shifts[1], value))
        for shift in range(3):
            for at, z in enumerate(layers):
                field[shift, z, pl.ds(1, INLINE)] = versions[shift][
                    at * layer : (at + 1) * layer
                ].reshape(INLINE, CROSS, width)

    def halo_pair(which):
        up = remote(
            edge.at[which, 0],
            halo.at[which, 1],
            halo_s.at[which, 0],
            halo_r.at[which, 0],
            {"seq": (me + count - 1) % count},
        )
        down = remote(
            edge.at[which, 1],
            halo.at[which, 0],
            halo_s.at[which, 1],
            halo_r.at[which, 1],
            {"seq": (me + 1) % count},
        )
        return (up, down)

    def halo_start(which, value):
        edge[which, 0] = value[:layer]
        edge[which, 1] = value[tokens_dev - layer :]
        up, down = halo_pair(which)

        @pl.when(me > 0)
        def _():
            up.start()

        @pl.when(me < count - 1)
        def _():
            down.start()

    def halo_finish(which, field):
        up, down = halo_pair(which)

        @pl.when(me > 0)
        def _():
            down.wait_recv()
            up.wait_send()

        @pl.when(me < count - 1)
        def _():
            up.wait_recv()
            down.wait_send()

        fill(field, (0, depth + 1), halo[which].reshape(2 * layer, width))

    def window(field, z, i, c, lanes):
        return field[c, pl.ds(z, depth), pl.ds(i, INLINE), :, lanes]

    def lanes_of(j):
        return pl.ds(pl.multiple_of(j * LANES, LANES), LANES)

    def convolve(field, flip, start, stop):
        def body(j, carry):
            lanes = lanes_of(j)
            result = window(field, 1, 1, 1, lanes)
            for offset in range(27):
                z, i, c = (offset // 9, offset // 3 % 3, offset % 3)
                if flip:
                    z, i, c = (2 - z, 2 - i, 2 - c)
                result = result + ker_ref[pl.ds(offset, 1), lanes] * window(field, z, i, c, lanes)
            cells[:, lanes] = result.reshape(tokens_dev, LANES).astype(jnp.bfloat16)
            return carry

        lax.fori_loop(start, stop, body, 0)

    def kernel_sums():
        def body(j, carry):
            lanes = lanes_of(j)
            grad = window(field_d, 1, 1, 1, lanes)
            for offset in range(27):
                z, i, c = (offset // 9, offset // 3 % 3, offset % 3)
                product = grad * window(field_x, z, i, c, lanes)
                sums[0, pl.ds(offset, 1), lanes] = jnp.sum(
                    product.reshape(tokens_dev, LANES), axis=0, keepdims=True
                )
            return carry

        lax.fori_loop(0, width // LANES, body, 0)

    tile = 2 * LANES
    chunks = width // LANES
    own_layers = tuple(range(1, depth + 1))

    def turn_body(n, carry):
        at = pl.multiple_of(n * LANES, LANES)
        turned[pl.ds(at, LANES), :] = (
            dp_ref[:, pl.ds(at, LANES)].astype(jnp.float32).T.astype(jnp.bfloat16)
        )
        return carry

    def back_chip(position):
        at = pl.ds(pl.multiple_of(at_ring(position) // 2 * (2 * rows), 16), 2 * rows)
        back_rows[at, :] = times(w_all[at, :], turned[...]).astype(jnp.bfloat16)

    def back_step(hop):
        for way in range(2):
            for copy in to_sibling.get((way, hop), ()):
                copy.wait_recv()
        if hop <= min(hops):
            back_chip(ring - hop)
        if hop > 0:
            back_chip(ring + hop)

    lax.fori_loop(0, w_ref.shape[1] // LANES, turn_body, 0)
    clear(field_x)
    clear(field_d)
    ring_step(1)
    move_x = exchange(0, tok_ref)
    back_step(0)
    ring_step(2)
    across_step(1)
    grid_x = times(to_cells, landed(0, move_x)).astype(jnp.bfloat16)
    halo_start(0, grid_x)
    fill(field_x, own_layers, grid_x)
    for hop in range(3, line + 1):
        ring_step(hop)
        across_step(hop - 1)
        back_step(hop - 2)
    halo_finish(0, field_x)
    back_step(line - 1)
    across_step(line)
    back_step(line)

    move_d = outgoing(
        2,
        lax.dot_general(
            same,
            back_rows[...],
            (((1,), (1,)), ((), ())),
            preferred_element_type=jnp.float32,
        ),
    )
    convolve(field_x, False, 0, chunks)
    move_y = outgoing(1, times(to_slots, cells[...]))

    grid_d = times(to_cells, landed(2, move_d)).astype(jnp.bfloat16)
    halo_start(1, grid_d)
    fill(field_d, own_layers, grid_d)
    sums[0, pl.ds(3 * CROSS, CROSS)] = jnp.zeros((CROSS, width), jnp.float32)
    kernel_sums()

    half, quarter = (2 * CROSS, CROSS)
    core_rows = pl.multiple_of(core * half, CROSS)
    far_core_rows = pl.multiple_of((1 - core) * half, CROSS)
    plane_rows = pl.multiple_of(plane * quarter, CROSS)
    far_plane_rows = pl.multiple_of((1 - plane) * quarter, CROSS)
    home = pl.multiple_of(core * half + plane * quarter, CROSS)
    partners = []
    bit = 2
    while bit < count:
        partners.append({"seq": me + bit - 2 * bit * (me // bit % 2)})
        bit *= 2
    stages = len(partners) + 4

    def sum_copy(stage):
        if stage == 0:
            src, dst = (sums.at[0, pl.ds(far_core_rows, half)], arrived.at[0, pl.ds(0, half)])
            target = {"seq": sibling}
        elif stage == 1:
            src, dst = (sums.at[1, pl.ds(far_plane_rows, quarter)], arrived.at[1, pl.ds(0, quarter)])
            target = {"dp": 1 - plane}
        elif stage < stages - 2:
            src, dst = (sums.at[stage, pl.ds(0, quarter)], arrived.at[stage, pl.ds(0, quarter)])
            target = partners[stage - 2]
        elif stage == stages - 2:
            src = dst = total.at[pl.ds(home, quarter)]
            target = {"dp": 1 - plane}
        else:
            src = dst = total.at[pl.ds(core_rows, half)]
            target = {"seq": sibling}
        copy = remote(src, dst, sum_s.at[stage], sum_r.at[stage], target)
        copy.start()
        sent.append(copy)
        return copy

    def sum_step(stage, copy):
        copy.wait_recv()
        if stage == 0:
            own = sums[0, pl.ds(core_rows, half)]
            sums[1, pl.ds(0, half)] = own + arrived[0, pl.ds(0, half)]
        elif stage < stages - 2:
            own = sums[stage, pl.ds(plane_rows if stage == 1 else 0, quarter)]
            added = own + arrived[stage, pl.ds(0, quarter)]
            if stage + 1 == stages - 2:
                total[pl.ds(home, quarter)] = added
            else:
                sums[stage + 1, pl.ds(0, quarter)] = added
        if stage + 1 < stages:
            return sum_copy(stage + 1)
        dker_ref[...] = total[: dker_ref.shape[0]]
        return copy

    summing = sum_copy(0)
    halo_finish(1, field_d)
    convolve(field_d, True, 0, chunks // 2)
    summing = sum_step(0, summing)
    convolve(field_d, True, chunks // 2, chunks)
    summing = sum_step(1, summing)
    move_b = outgoing(3, times(to_slots, cells[...]))
    summing = sum_step(2, summing)

    rows_y = landed(1, move_y)
    tiles = w_ref.shape[1] // tile

    def front_body(n, carry):
        at = pl.multiple_of(n * tile, tile)
        proj_ref[:, pl.ds(at, tile)] = times(rows_y, w_all[:, pl.ds(at, tile)]).astype(
            jnp.bfloat16
        )
        return carry

    for stage in range(3, stages):
        low, high = [tiles * part // (stages - 3) for part in (stage - 3, stage - 2)]
        lax.fori_loop(low, high, front_body, 0)
        summing = sum_step(stage, summing)
    dtok_ref[...] = landed(3, move_b)
    for copy in sent:
        copy.wait_send()


def fused_shards(tokens, place, kernel, proj_weight, d_projected):
    count = lax.axis_size("seq")
    tokens_dev, width = tokens.shape[1:]
    columns = proj_weight.shape[1]
    layer = INLINE * CROSS
    group = tokens_dev // count
    depth = tokens_dev // layer
    stages = count.bit_length() + 2
    line = count // 4
    taps = kernel.shape[0]
    vmem = pl.BlockSpec(memory_space=pltpu.VMEM)
    dma = pltpu.SemaphoreType.DMA
    bf16, f32 = (jnp.bfloat16, jnp.float32)
    projected, d_tokens, d_kernel = pl.pallas_call(
        functools.partial(fused, count),
        out_shape=(
            jax.ShapeDtypeStruct((tokens_dev, columns), bf16),
            jax.ShapeDtypeStruct((tokens_dev, width), bf16),
            jax.ShapeDtypeStruct((taps, width), f32),
        ),
        in_specs=[vmem] * 5,
        out_specs=(vmem, vmem, vmem),
        scratch_shapes=[
            pltpu.VMEM((width, columns), bf16),
            pltpu.VMEM((4, count, group, width), bf16),
            pltpu.VMEM((4, count, group, width), bf16),
            pltpu.VMEM((2, 2, layer, width), bf16),
            pltpu.VMEM((2, 2, layer, width), bf16),
            pltpu.VMEM((3, depth + 2, INLINE + 2, CROSS, width), f32),
            pltpu.VMEM((3, depth + 2, INLINE + 2, CROSS, width), f32),
            pltpu.VMEM((tokens_dev, width), bf16),
            pltpu.VMEM((columns, tokens_dev), bf16),
            pltpu.VMEM((width, tokens_dev), bf16),
            pltpu.VMEM((stages, 4 * CROSS, width), f32),
            pltpu.VMEM((stages, 4 * CROSS, width), f32),
            pltpu.VMEM((4 * CROSS, width), f32),
            dma((4, count)),
            dma((4, count)),
            dma((2, line + 1, 2)),
            dma((2, line + 1, 2)),
            dma((2, line + 1)),
            dma((2, line + 1)),
            dma((3, line + 1, 3)),
            dma((3, line + 1, 3)),
            dma((2, 2)),
            dma((2, 2)),
            dma((stages,)),
            dma((stages,)),
        ],
        compiler_params=pltpu.CompilerParams(
            collective_id=0, has_side_effects=True, vmem_limit_bytes=56 * 1024 * 1024
        ),
        cost_estimate=pl.CostEstimate(
            flops=4 * tokens_dev * width * columns,
            bytes_accessed=4 * tokens_dev * columns,
            transcendentals=0,
        ),
    )(
        tokens[0].reshape(count, group, width),
        place,
        kernel,
        proj_weight,
        d_projected[0],
    )
    return (projected[None], d_tokens[None], d_kernel)


def solution(mesh):
    placed = (P("dp", "seq", None), P("seq", None), P(), P("seq", None), P("dp", "seq", None))
    count = mesh.shape["seq"]
    use_kernel = mesh.shape["dp"] == 2 and count == 16
    return jax.shard_map(
        fused_shards if use_kernel else shards,
        mesh=mesh,
        in_specs=placed,
        out_specs=(P("dp", "seq", None), P("dp", "seq", None), P()),
        check_vma=False,
    )
```

```python
import functools

import jax
import jax.numpy as jnp
from jax import lax
from jax.experimental import pallas as pl
from jax.experimental.pallas import tpu as pltpu
from jax.sharding import PartitionSpec as P

INLINE = 8
CROSS = 8
MESH = pl.DeviceIdType.MESH
LANES = 128


def with_halo(value, sides, width):
    for axis, dim in sides:
        size, length = (lax.axis_size(axis), value.shape[dim])
        up = [(i, (i + 1) % size) for i in range(size - 1)]
        down = [(j, i) for i, j in up]
        last = lax.slice_in_dim(value, length - width, length, axis=dim)
        first = lax.slice_in_dim(value, 0, width, axis=dim)
        before = lax.ppermute(last, axis, up)
        after = lax.ppermute(first, axis, down)
        value = jnp.concatenate([before, value, after], axis=dim)
    return value


def brick_cells(landed, inverse):
    tokens_dev = inverse.shape[0]
    width = landed.shape[-1]
    slots = landed.reshape(tokens_dev, width)
    cells = jnp.take(slots, inverse, axis=0)
    return cells.reshape(tokens_dev // (INLINE * CROSS), INLINE, CROSS, width)


def scan_pieces(cells, order, count):
    width = cells.shape[-1]
    tokens_dev = order.shape[0]
    slots = jnp.take(cells.reshape(tokens_dev, width), order, axis=0)
    return slots.reshape(count, tokens_dev // count, width)


def to_bricks(rows, inverse, count):
    tokens_dev, width = rows.shape
    landed = lax.all_to_all(
        rows.reshape(count, tokens_dev // count, width),
        "seq",
        split_axis=0,
        concat_axis=0,
        tiled=True,
    )
    return brick_cells(landed, inverse)


def to_scan(cells, order, count):
    landed = lax.all_to_all(
        scan_pieces(cells, order, count), "seq", split_axis=0, concat_axis=0, tiled=True
    )
    return landed.reshape(order.shape[0], cells.shape[-1])


def with_faces(block):
    deeper = with_halo(block, (("seq", 0),), 1)
    return jnp.pad(deeper, ((0, 0), (1, 1), (1, 1), (0, 0)))


def window(field, depth_dev, start_z, start_i, start_c):
    return field[
        start_z : start_z + depth_dev, start_i : start_i + INLINE, start_c : start_c + CROSS
    ].astype(jnp.float32)


def forward_conv(grid_x, pad_x, kernel, depth_dev):
    conv = jnp.zeros(grid_x.shape, jnp.float32)
    for offset in range(27):
        conv = conv + kernel[offset] * window(
            pad_x, depth_dev, offset // 9, offset // 3 % 3, offset % 3
        )
    return (grid_x.astype(jnp.float32) + conv).astype(jnp.bfloat16)


def backward_conv(grid_d, pad_d, pad_x, kernel, depth_dev):
    grid_float = grid_d.astype(jnp.float32)
    back = grid_float
    partial_value = []
    for offset in range(27):
        dz, di, dc = (offset // 9, offset // 3 % 3, offset % 3)
        back = back + kernel[offset] * window(pad_d, depth_dev, 2 - dz, 2 - di, 2 - dc)
        partial_value.append(
            jnp.sum(grid_float * window(pad_x, depth_dev, dz, di, dc), axis=(0, 1, 2))
        )
    return (back.astype(jnp.bfloat16), jnp.stack(partial_value))


def shards(tokens, place, kernel, proj_weight, d_projected):
    count = lax.axis_size("seq")
    order = place[0]
    inverse = jnp.argsort(order)
    rows_x = tokens[0]
    d_rows = d_projected[0]
    depth_dev = rows_x.shape[0] // (INLINE * CROSS)
    d_y = lax.dot_general(
        d_rows,
        lax.all_gather(proj_weight, "seq", axis=0, tiled=True),
        (((1,), (1,)), ((), ())),
        preferred_element_type=jnp.float32,
    )
    d_y = d_y.astype(jnp.bfloat16)
    grid_x = to_bricks(rows_x, inverse, count)
    pad_x = with_faces(grid_x)
    grid_y = forward_conv(grid_x, pad_x, kernel, depth_dev)
    rows_y = to_scan(grid_y, order, count)
    grid_d = to_bricks(d_y, inverse, count)
    pad_d = with_faces(grid_d)
    back, partial_value = backward_conv(grid_d, pad_d, pad_x, kernel, depth_dev)
    d_tokens = to_scan(back, order, count)
    projected = jnp.dot(
        rows_y,
        lax.all_gather(proj_weight, "seq", axis=0, tiled=True),
        preferred_element_type=jnp.float32,
    )
    projected = projected.astype(jnp.bfloat16)
    d_kernel = lax.psum(partial_value, ("dp", "seq"))
    return (projected[None], d_tokens[None], d_kernel)


def fused(
    count,
    tok_ref,
    row_ref,
    ker_ref,
    w_ref,
    dp_ref,
    proj_ref,
    dtok_ref,
    dker_ref,
    w_all,
    land,
    send,
    edge,
    halo,
    field_x,
    field_d,
    cells,
    turned,
    back_rows,
    sums,
    arrived,
    paired,
    layers,
    total,
    move_s,
    move_r,
    ring_s,
    ring_r,
    part_s,
    part_r,
    sib_s,
    sib_r,
    halo_s,
    halo_r,
    sum_s,
    sum_r,
):
    me = lax.axis_index("seq")
    plane = lax.axis_index("dp")
    tokens_dev, width = cells.shape
    rows = w_ref.shape[0]
    third = w_ref.shape[1] // 3
    layer = INLINE * CROSS
    depth = tokens_dev // layer
    group = tokens_dev // count
    chips = count // 2
    line = chips // 2
    core = me % 2
    chip = me // 2
    chip_y = chip % 2
    chip_z = chip // 2
    ring = chip_z * (1 - chip_y) + (chips - 1 - chip_z) * chip_y
    sibling = me + 1 - 2 * core
    sign = 1 - 2 * core
    own_third = pl.multiple_of((1 + plane) * third, LANES)
    other_third = pl.multiple_of((2 - plane) * third, LANES)

    def at_ring(position):
        spot = (position + 2 * chips) % chips
        side = spot // line
        z = spot * (1 - side) + (chips - 1 - spot) * side
        return (z * 2 + side) * 2 + core

    def block(shard, start):
        return w_all.at[pl.ds(pl.multiple_of(shard * rows, 16), rows), pl.ds(start, third)]

    def whole(shard):
        return w_all.at[pl.ds(pl.multiple_of(shard * rows, 16), rows), :]

    def remote(src, dst, s_sem, r_sem, target):
        return pltpu.make_async_remote_copy(
            src_ref=src,
            dst_ref=dst,
            send_sem=s_sem,
            recv_sem=r_sem,
            device_id=target,
            device_id_type=MESH,
        )

    edge_zero = jnp.zeros((layer, width), jnp.bfloat16)
    for which in range(2):
        for side in range(2):
            halo[which, side] = edge_zero
    w_all[pl.ds(pl.multiple_of(me * rows, 16), rows), :] = w_ref[...]

    barrier = pltpu.get_barrier_semaphore()
    for step in range(1, count):
        pl.semaphore_signal(
            barrier, inc=1, device_id={"seq": (me + step) % count}, device_id_type=MESH
        )
    pl.semaphore_signal(barrier, inc=1, device_id={"dp": 1 - plane}, device_id_type=MESH)
    pl.semaphore_signal(
        barrier, inc=1, device_id={"dp": 1 - plane, "seq": sibling}, device_id_type=MESH
    )
    pl.semaphore_wait(barrier, count + 1)

    sent = []

    def exchange(which, source):
        copies = []
        for step in range(1, count):
            target = (me + step) % count
            copies.append(
                remote(
                    source.at[target],
                    land.at[which, me],
                    move_s.at[which, step],
                    move_r.at[which, step],
                    {"seq": target},
                )
            )
        for copy in copies:
            copy.start()
        sent.extend(copies)
        land[which, pl.ds(me, 1)] = source[pl.ds(me, 1)]
        return copies

    def landed(which, copies):
        for copy in copies:
            copy.wait_recv()
        value = land[which].astype(jnp.float32)
        return value.reshape(tokens_dev, width).astype(jnp.bfloat16)

    def outgoing(which, slots):
        send[which] = slots.reshape(count, group, width).astype(jnp.bfloat16)
        return exchange(which, send.at[which])

    hops = (line, chips - 1 - line)
    signs = (sign, -sign)

    def ring_copies(way, hop):
        shard = at_ring(ring - signs[way] * (hop - 1))
        target = {"seq": at_ring(ring + signs[way])}
        pair = []
        for piece, start in enumerate((0, own_third)):
            pair.append(
                remote(
                    block(shard, start),
                    block(shard, start),
                    ring_s.at[way, hop, piece],
                    ring_r.at[way, hop, piece],
                    target,
                )
            )
        return pair

    moving = {}
    for way in range(2):
        moving[way, 1] = ring_copies(way, 1)
    for piece in (1, 0):
        for way in range(2):
            moving[way, 1][piece].start()
    for way in range(2):
        sent.extend(moving[way, 1])
    own_copy = remote(
        whole(me), whole(me), sib_s.at[0, 0, 0], sib_r.at[0, 0, 0], {"seq": sibling}
    )
    own_copy.start()
    sent.append(own_copy)
    to_sibling = {(0, 0): [own_copy]}
    across = {}

    def sibling_copy(way, hop, piece, shard, start):
        copy = remote(
            block(shard, start),
            block(shard, start),
            sib_s.at[1 + way, hop, piece],
            sib_r.at[1 + way, hop, piece],
            {"seq": sibling},
        )
        copy.start()
        sent.append(copy)
        to_sibling.setdefault((way, hop), []).append(copy)

    def ring_step(hop):
        ways = [way for way in range(2) if hop <= hops[way]]
        for way in ways:
            if hop < hops[way]:
                moving[way, hop + 1] = ring_copies(way, hop + 1)
                sent.extend(moving[way, hop + 1])
        for piece, start in ((1, own_third), (0, 0)):
            for way in ways:
                shard = at_ring(ring - signs[way] * hop)
                moving[way, hop][piece].wait_recv()
                if hop < hops[way]:
                    moving[way, hop + 1][piece].start()
                if piece == 1:
                    copy = remote(
                        block(shard, start),
                        block(shard, start),
                        part_s.at[way, hop],
                        part_r.at[way, hop],
                        {"dp": 1 - plane},
                    )
                    copy.start()
                    sent.append(copy)
                    across[way, hop] = copy
                sibling_copy(way, hop, piece, shard, start)

    def across_step(hop):
        for way in range(2):
            if hop <= hops[way]:
                shard = at_ring(ring - signs[way] * hop)
                across[way, hop].wait_recv()
                sibling_copy(way, hop, 2, shard, other_third)

    square = (tokens_dev, tokens_dev)
    first = lax.broadcasted_iota(jnp.int32, square, 0)
    second = lax.broadcasted_iota(jnp.int32, square, 1)

    def ones_where(mask):
        return jnp.where(mask, 1.0, 0.0).astype(jnp.bfloat16)

    chosen = jnp.where(jnp.broadcast_to(row_ref[...], square) == first, 1.0, 0.0)
    to_cells = chosen.astype(jnp.bfloat16)
    to_slots = chosen.T.astype(jnp.bfloat16)
    same = ones_where(first == second)
    spot = first % CROSS
    shifts = (
        ones_where((second == first - 1) & (spot > 0)),
        ones_where((second == first + 1) & (spot < CROSS - 1)),
    )

    def times(left, right):
        return jnp.dot(left, right, preferred_element_type=jnp.float32)

    def clear(field):
        pad = jnp.zeros((CROSS, width), jnp.float32)
        for shift in range(3):
            for z in range(depth + 2):
                field[shift, z, 0] = pad
                field[shift, z, INLINE + 1] = pad

    def fill(field, layers, value):
        versions = (times(shifts[0], value), value.astype(jnp.float32), times(shifts[1], value))
        for shift in range(3):
            for at, z in enumerate(layers):
                field[shift, z, pl.ds(1, INLINE)] = versions[shift][
                    at * layer : (at + 1) * layer
                ].reshape(INLINE, CROSS, width)

    def halo_pair(which):
        up = remote(
            edge.at[which, 0],
            halo.at[which, 1],
            halo_s.at[which, 0],
            halo_r.at[which, 0],
            {"seq": (me + count - 1) % count},
        )
        down = remote(
            edge.at[which, 1],
            halo.at[which, 0],
            halo_s.at[which, 1],
            halo_r.at[which, 1],
            {"seq": (me + 1) % count},
        )
        return (up, down)

    def halo_start(which, value):
        edge[which, 0] = value[:layer]
        edge[which, 1] = value[tokens_dev - layer :]
        up, down = halo_pair(which)

        @pl.when(me > 0)
        def _():
            up.start()

        @pl.when(me < count - 1)
        def _():
            down.start()

    def halo_finish(which, field):
        up, down = halo_pair(which)

        @pl.when(me > 0)
        def _():
            down.wait_recv()
            up.wait_send()

        @pl.when(me < count - 1)
        def _():
            up.wait_recv()
            down.wait_send()

        fill(field, (0, depth + 1), halo[which].reshape(2 * layer, width))

    def window(field, z, i, c, lanes):
        return field[c, pl.ds(z, depth), pl.ds(i, INLINE), :, lanes]

    def lanes_of(j):
        return pl.ds(pl.multiple_of(j * LANES, LANES), LANES)

    def convolve(field, flip, start, stop):
        def body(j, carry):
            lanes = lanes_of(j)
            result = window(field, 1, 1, 1, lanes)
            for offset in range(27):
                z, i, c = (offset // 9, offset // 3 % 3, offset % 3)
                if flip:
                    z, i, c = (2 - z, 2 - i, 2 - c)
                result = result + ker_ref[pl.ds(offset, 1), lanes] * window(field, z, i, c, lanes)
            cells[:, lanes] = result.reshape(tokens_dev, LANES).astype(jnp.bfloat16)
            return carry

        lax.fori_loop(start, stop, body, 0)

    def kernel_sums():
        def body(j, carry):
            lanes = lanes_of(j)
            grad = window(field_d, 1, 1, 1, lanes)
            for offset in range(27):
                z, i, c = (offset // 9, offset // 3 % 3, offset % 3)
                product = grad * window(field_x, z, i, c, lanes)
                sums[pl.ds(offset, 1), lanes] = jnp.sum(
                    product.reshape(tokens_dev, LANES), axis=0, keepdims=True
                )
            return carry

        lax.fori_loop(0, width // LANES, body, 0)

    tile = 2 * LANES
    chunks = width // LANES
    own_layers = tuple(range(1, depth + 1))

    def turn_body(n, carry):
        at = pl.multiple_of(n * LANES, LANES)
        turned[pl.ds(at, LANES), :] = (
            dp_ref[:, pl.ds(at, LANES)].astype(jnp.float32).T.astype(jnp.bfloat16)
        )
        return carry

    def back_chip(position):
        at = pl.ds(pl.multiple_of(at_ring(position) // 2 * (2 * rows), 16), 2 * rows)
        back_rows[at, :] = times(w_all[at, :], turned[...]).astype(jnp.bfloat16)

    def back_step(hop):
        for way in range(2):
            for copy in to_sibling.get((way, hop), ()):
                copy.wait_recv()
        if hop <= min(hops):
            back_chip(ring - hop)
        if hop > 0:
            back_chip(ring + hop)

    lax.fori_loop(0, w_ref.shape[1] // LANES, turn_body, 0)
    clear(field_x)
    clear(field_d)
    ring_step(1)
    move_x = exchange(0, tok_ref)
    back_step(0)
    ring_step(2)
    across_step(1)
    grid_x = times(to_cells, landed(0, move_x)).astype(jnp.bfloat16)
    halo_start(0, grid_x)
    fill(field_x, own_layers, grid_x)
    for hop in range(3, line + 1):
        ring_step(hop)
        across_step(hop - 1)
        back_step(hop - 2)
    halo_finish(0, field_x)
    back_step(line - 1)
    across_step(line)
    back_step(line)

    move_d = outgoing(
        2,
        lax.dot_general(
            same,
            back_rows[...],
            (((1,), (1,)), ((), ())),
            preferred_element_type=jnp.float32,
        ),
    )
    convolve(field_x, False, 0, chunks)
    move_y = outgoing(1, times(to_slots, cells[...]))

    grid_d = times(to_cells, landed(2, move_d)).astype(jnp.bfloat16)
    halo_start(1, grid_d)
    fill(field_d, own_layers, grid_d)
    sums[pl.ds(3 * CROSS, CROSS)] = jnp.zeros((CROSS, width), jnp.float32)
    kernel_sums()

    def start_all(copies):
        for copy in copies:
            copy.start()
        sent.extend(copies)
        return copies

    def part_rows(core_at, plane_at):
        return pl.ds(pl.multiple_of((core_at * 2 + plane_at) * CROSS, CROSS), CROSS)

    home = part_rows(core, plane)
    squad = (
        (1 - core, plane, {"seq": sibling}),
        (core, 1 - plane, {"dp": 1 - plane}),
        (1 - core, 1 - plane, {"dp": 1 - plane, "seq": sibling}),
    )

    def scatter_sums():
        return start_all(
            [
                remote(
                    sums.at[part_rows(core_at, plane_at)],
                    arrived.at[k],
                    sum_s.at[0, k],
                    sum_r.at[0, k],
                    target,
                )
                for k, (core_at, plane_at, target) in enumerate(squad)
            ]
        )

    def pair_sums(copies):
        for copy in copies:
            copy.wait_recv()
        paired[...] = sums[home] + arrived[0] + arrived[1] + arrived[2]
        target = {"seq": me + 2 - 4 * chip_y}
        return start_all([remote(paired, arrived.at[3], sum_s.at[1, 0], sum_r.at[1, 0], target)])

    def line_sums(copies):
        for copy in copies:
            copy.wait_recv()
        layers[chip_z] = paired[...] + arrived[3]
        return start_all(
            [
                remote(
                    layers.at[chip_z],
                    layers.at[chip_z],
                    sum_s.at[2, k],
                    sum_r.at[2, k],
                    {"seq": (chip_z + k) % line * 4 + chip_y * 2 + core},
                )
                for k in range(1, line)
            ]
        )

    def share_sums(copies):
        for copy in copies:
            copy.wait_recv()
        whole_sum = layers[0]
        for k in range(1, line):
            whole_sum = whole_sum + layers[k]
        total[home] = whole_sum
        return start_all(
            [
                remote(total.at[home], total.at[home], sum_s.at[3, k], sum_r.at[3, k], target)
                for k, (core_at, plane_at, target) in enumerate(squad)
            ]
        )

    def finish_sums(copies):
        for copy in copies:
            copy.wait_recv()
        dker_ref[...] = total[: dker_ref.shape[0]]

    summing = scatter_sums()
    halo_finish(1, field_d)
    convolve(field_d, True, 0, chunks // 2)
    summing = pair_sums(summing)
    convolve(field_d, True, chunks // 2, chunks)
    summing = line_sums(summing)
    move_b = outgoing(3, times(to_slots, cells[...]))

    rows_y = landed(1, move_y)
    tiles = w_ref.shape[1] // tile

    def front_body(n, carry):
        at = pl.multiple_of(n * tile, tile)
        proj_ref[:, pl.ds(at, tile)] = times(rows_y, w_all[:, pl.ds(at, tile)]).astype(
            jnp.bfloat16
        )
        return carry

    lax.fori_loop(0, tiles // 2, front_body, 0)
    summing = share_sums(summing)
    lax.fori_loop(tiles // 2, tiles, front_body, 0)
    finish_sums(summing)
    dtok_ref[...] = landed(3, move_b)
    for copy in sent:
        copy.wait_send()


def copy_results(proj_in, dtok_in, dker_in, proj_out, dtok_out, dker_out, sems):
    half = pl.ds(0, proj_in.shape[0] // 2)
    rest = pl.ds(proj_in.shape[0] // 2, proj_in.shape[0] // 2)
    pairs = (
        (proj_in.at[half], proj_out.at[half]),
        (proj_in.at[rest], proj_out.at[rest]),
        (dtok_in, dtok_out),
        (dker_in, dker_out),
    )
    copies = [pltpu.make_async_copy(src, dst, sems.at[k]) for k, (src, dst) in enumerate(pairs)]
    for copy in copies:
        copy.start()
    for copy in copies:
        copy.wait()


def fused_shards(tokens, place, kernel, proj_weight, d_projected):
    count = lax.axis_size("seq")
    tokens_dev, width = tokens.shape[1:]
    columns = proj_weight.shape[1]
    layer = INLINE * CROSS
    group = tokens_dev // count
    depth = tokens_dev // layer
    line = count // 4
    taps = kernel.shape[0]
    vmem = pl.BlockSpec(memory_space=pltpu.VMEM)
    dma = pltpu.SemaphoreType.DMA
    bf16, f32 = (jnp.bfloat16, jnp.float32)
    projected, d_tokens, d_kernel = pl.pallas_call(
        functools.partial(fused, count),
        out_shape=(
            jax.ShapeDtypeStruct((tokens_dev, columns), bf16),
            jax.ShapeDtypeStruct((tokens_dev, width), bf16),
            jax.ShapeDtypeStruct((taps, width), f32),
        ),
        in_specs=[vmem] * 5,
        out_specs=(vmem, vmem, vmem),
        scratch_shapes=[
            pltpu.VMEM((width, columns), bf16),
            pltpu.VMEM((4, count, group, width), bf16),
            pltpu.VMEM((4, count, group, width), bf16),
            pltpu.VMEM((2, 2, layer, width), bf16),
            pltpu.VMEM((2, 2, layer, width), bf16),
            pltpu.VMEM((3, depth + 2, INLINE + 2, CROSS, width), f32),
            pltpu.VMEM((3, depth + 2, INLINE + 2, CROSS, width), f32),
            pltpu.VMEM((tokens_dev, width), bf16),
            pltpu.VMEM((columns, tokens_dev), bf16),
            pltpu.VMEM((width, tokens_dev), bf16),
            pltpu.VMEM((4 * CROSS, width), f32),
            pltpu.VMEM((4, CROSS, width), f32),
            pltpu.VMEM((CROSS, width), f32),
            pltpu.VMEM((line, CROSS, width), f32),
            pltpu.VMEM((4 * CROSS, width), f32),
            dma((4, count)),
            dma((4, count)),
            dma((2, line + 1, 2)),
            dma((2, line + 1, 2)),
            dma((2, line + 1)),
            dma((2, line + 1)),
            dma((3, line + 1, 3)),
            dma((3, line + 1, 3)),
            dma((2, 2)),
            dma((2, 2)),
            dma((4, 4)),
            dma((4, 4)),
        ],
        compiler_params=pltpu.CompilerParams(
            collective_id=0, has_side_effects=True, vmem_limit_bytes=56 * 1024 * 1024
        ),
        cost_estimate=pl.CostEstimate(
            flops=4 * tokens_dev * width * columns,
            bytes_accessed=4 * tokens_dev * columns,
            transcendentals=0,
        ),
    )(
        tokens[0].reshape(count, group, width),
        place,
        kernel,
        proj_weight,
        d_projected[0],
    )
    results = [projected, d_tokens, d_kernel]
    anywhere = pl.BlockSpec(memory_space=pl.ANY)
    projected, d_tokens, d_kernel = pl.pallas_call(
        copy_results,
        out_shape=tuple(jax.ShapeDtypeStruct(r.shape, r.dtype) for r in results),
        in_specs=[anywhere] * 3,
        out_specs=(anywhere,) * 3,
        scratch_shapes=[dma((4,))],
    )(*results)
    return (projected[None], d_tokens[None], d_kernel)


def solution(mesh):
    placed = (P("dp", "seq", None), P("seq", None), P(), P("seq", None), P("dp", "seq", None))
    count = mesh.shape["seq"]
    use_kernel = mesh.shape["dp"] == 2 and count == 16
    return jax.shard_map(
        fused_shards if use_kernel else shards,
        mesh=mesh,
        in_specs=placed,
        out_specs=(P("dp", "seq", None), P("dp", "seq", None), P()),
        check_vma=False,
    )
```

```python
import functools

import jax
import jax.numpy as jnp
from jax import lax
from jax.experimental import pallas as pl
from jax.experimental.pallas import tpu as pltpu
from jax.sharding import PartitionSpec as P

INLINE = 8
CROSS = 8
MESH = pl.DeviceIdType.MESH
LANES = 128


def with_halo(value, sides, width):
    for axis, dim in sides:
        size, length = (lax.axis_size(axis), value.shape[dim])
        up = [(i, (i + 1) % size) for i in range(size - 1)]
        down = [(j, i) for i, j in up]
        last = lax.slice_in_dim(value, length - width, length, axis=dim)
        first = lax.slice_in_dim(value, 0, width, axis=dim)
        before = lax.ppermute(last, axis, up)
        after = lax.ppermute(first, axis, down)
        value = jnp.concatenate([before, value, after], axis=dim)
    return value


def brick_cells(landed, inverse):
    tokens_dev = inverse.shape[0]
    width = landed.shape[-1]
    slots = landed.reshape(tokens_dev, width)
    cells = jnp.take(slots, inverse, axis=0)
    return cells.reshape(tokens_dev // (INLINE * CROSS), INLINE, CROSS, width)


def scan_pieces(cells, order, count):
    width = cells.shape[-1]
    tokens_dev = order.shape[0]
    slots = jnp.take(cells.reshape(tokens_dev, width), order, axis=0)
    return slots.reshape(count, tokens_dev // count, width)


def to_bricks(rows, inverse, count):
    tokens_dev, width = rows.shape
    landed = lax.all_to_all(
        rows.reshape(count, tokens_dev // count, width),
        "seq",
        split_axis=0,
        concat_axis=0,
        tiled=True,
    )
    return brick_cells(landed, inverse)


def to_scan(cells, order, count):
    landed = lax.all_to_all(
        scan_pieces(cells, order, count), "seq", split_axis=0, concat_axis=0, tiled=True
    )
    return landed.reshape(order.shape[0], cells.shape[-1])


def with_faces(block):
    deeper = with_halo(block, (("seq", 0),), 1)
    return jnp.pad(deeper, ((0, 0), (1, 1), (1, 1), (0, 0)))


def window(field, depth_dev, start_z, start_i, start_c):
    return field[
        start_z : start_z + depth_dev, start_i : start_i + INLINE, start_c : start_c + CROSS
    ].astype(jnp.float32)


def forward_conv(grid_x, pad_x, kernel, depth_dev):
    conv = jnp.zeros(grid_x.shape, jnp.float32)
    for offset in range(27):
        conv = conv + kernel[offset] * window(
            pad_x, depth_dev, offset // 9, offset // 3 % 3, offset % 3
        )
    return (grid_x.astype(jnp.float32) + conv).astype(jnp.bfloat16)


def backward_conv(grid_d, pad_d, pad_x, kernel, depth_dev):
    grid_float = grid_d.astype(jnp.float32)
    back = grid_float
    partial_value = []
    for offset in range(27):
        dz, di, dc = (offset // 9, offset // 3 % 3, offset % 3)
        back = back + kernel[offset] * window(pad_d, depth_dev, 2 - dz, 2 - di, 2 - dc)
        partial_value.append(
            jnp.sum(grid_float * window(pad_x, depth_dev, dz, di, dc), axis=(0, 1, 2))
        )
    return (back.astype(jnp.bfloat16), jnp.stack(partial_value))


def shards(tokens, place, kernel, proj_weight, d_projected):
    count = lax.axis_size("seq")
    order = place[0]
    inverse = jnp.argsort(order)
    rows_x = tokens[0]
    d_rows = d_projected[0]
    depth_dev = rows_x.shape[0] // (INLINE * CROSS)
    d_y = lax.dot_general(
        d_rows,
        lax.all_gather(proj_weight, "seq", axis=0, tiled=True),
        (((1,), (1,)), ((), ())),
        preferred_element_type=jnp.float32,
    )
    d_y = d_y.astype(jnp.bfloat16)
    grid_x = to_bricks(rows_x, inverse, count)
    pad_x = with_faces(grid_x)
    grid_y = forward_conv(grid_x, pad_x, kernel, depth_dev)
    rows_y = to_scan(grid_y, order, count)
    grid_d = to_bricks(d_y, inverse, count)
    pad_d = with_faces(grid_d)
    back, partial_value = backward_conv(grid_d, pad_d, pad_x, kernel, depth_dev)
    d_tokens = to_scan(back, order, count)
    projected = jnp.dot(
        rows_y,
        lax.all_gather(proj_weight, "seq", axis=0, tiled=True),
        preferred_element_type=jnp.float32,
    )
    projected = projected.astype(jnp.bfloat16)
    d_kernel = lax.psum(partial_value, ("dp", "seq"))
    return (projected[None], d_tokens[None], d_kernel)


def fused(
    count,
    tok_ref,
    row_ref,
    ker_ref,
    w_ref,
    dp_ref,
    proj_ref,
    dtok_ref,
    dker_ref,
    w_all,
    land,
    send,
    edge,
    halo,
    field_x,
    field_d,
    cells,
    turned,
    back_rows,
    sums,
    arrived,
    paired,
    layers,
    total,
    move_s,
    move_r,
    ring_s,
    ring_r,
    part_s,
    part_r,
    sib_s,
    sib_r,
    halo_s,
    halo_r,
    sum_s,
    sum_r,
):
    me = lax.axis_index("seq")
    plane = lax.axis_index("dp")
    tokens_dev, width = cells.shape
    rows = w_ref.shape[0]
    third = w_ref.shape[1] // 3
    layer = INLINE * CROSS
    depth = tokens_dev // layer
    group = tokens_dev // count
    chips = count // 2
    line = chips // 2
    core = me % 2
    chip = me // 2
    chip_y = chip % 2
    chip_z = chip // 2
    ring = chip_z * (1 - chip_y) + (chips - 1 - chip_z) * chip_y
    sibling = me + 1 - 2 * core
    sign = 1 - 2 * core
    own_third = pl.multiple_of((1 + plane) * third, LANES)
    other_third = pl.multiple_of((2 - plane) * third, LANES)

    def at_ring(position):
        spot = (position + 2 * chips) % chips
        side = spot // line
        z = spot * (1 - side) + (chips - 1 - spot) * side
        return (z * 2 + side) * 2 + core

    upper = (rows // 32 + rows // 16 % 2) * 16
    halves = ((0, upper), (upper, rows - upper))

    def block(shard, start, half):
        low, size = halves[half]
        return w_all.at[pl.ds(pl.multiple_of(shard * rows + low, 16), size), pl.ds(start, third)]

    def whole(shard):
        return w_all.at[pl.ds(pl.multiple_of(shard * rows, 16), rows), :]

    def remote(src, dst, s_sem, r_sem, target):
        return pltpu.make_async_remote_copy(
            src_ref=src,
            dst_ref=dst,
            send_sem=s_sem,
            recv_sem=r_sem,
            device_id=target,
            device_id_type=MESH,
        )

    edge_zero = jnp.zeros((layer, width), jnp.bfloat16)
    for which in range(2):
        for side in range(2):
            halo[which, side] = edge_zero
    w_all[pl.ds(pl.multiple_of(me * rows, 16), rows), :] = w_ref[...]

    barrier = pltpu.get_barrier_semaphore()
    for step in range(1, count):
        pl.semaphore_signal(
            barrier, inc=1, device_id={"seq": (me + step) % count}, device_id_type=MESH
        )
    pl.semaphore_signal(barrier, inc=1, device_id={"dp": 1 - plane}, device_id_type=MESH)
    pl.semaphore_signal(
        barrier, inc=1, device_id={"dp": 1 - plane, "seq": sibling}, device_id_type=MESH
    )
    pl.semaphore_wait(barrier, count + 1)

    sent = []

    def exchange(which, source):
        copies = []
        for step in range(1, count):
            target = (me + step) % count
            copies.append(
                remote(
                    source.at[target],
                    land.at[which, me],
                    move_s.at[which, step],
                    move_r.at[which, step],
                    {"seq": target},
                )
            )
        for copy in copies:
            copy.start()
        sent.extend(copies)
        land[which, pl.ds(me, 1)] = source[pl.ds(me, 1)]
        return copies

    def landed(which, copies):
        for copy in copies:
            copy.wait_recv()
        value = land[which].astype(jnp.float32)
        return value.reshape(tokens_dev, width).astype(jnp.bfloat16)

    def outgoing(which, slots):
        send[which] = slots.reshape(count, group, width).astype(jnp.bfloat16)
        return exchange(which, send.at[which])

    hops = (line, chips - 1 - line)
    pieces = ((own_third, 0), (own_third, 1), (0, 0), (0, 1))
    signs = (sign, -sign)

    def ring_copies(way, hop):
        shard = at_ring(ring - signs[way] * (hop - 1))
        target = {"seq": at_ring(ring + signs[way])}
        pair = []
        for piece, (start, half) in enumerate(pieces):
            pair.append(
                remote(
                    block(shard, start, half),
                    block(shard, start, half),
                    ring_s.at[way, hop, piece],
                    ring_r.at[way, hop, piece],
                    target,
                )
            )
        return pair

    moving = {}
    for way in range(2):
        moving[way, 1] = ring_copies(way, 1)
    for piece in range(len(pieces)):
        for way in range(2):
            moving[way, 1][piece].start()
    for way in range(2):
        sent.extend(moving[way, 1])
    own_copy = remote(
        whole(me), whole(me), sib_s.at[0, 0, 0], sib_r.at[0, 0, 0], {"seq": sibling}
    )
    own_copy.start()
    sent.append(own_copy)
    to_sibling = {(0, 0): [own_copy]}
    across = {}

    def sibling_copy(way, hop, piece, shard, start, half):
        copy = remote(
            block(shard, start, half),
            block(shard, start, half),
            sib_s.at[1 + way, hop, piece],
            sib_r.at[1 + way, hop, piece],
            {"seq": sibling},
        )
        copy.start()
        sent.append(copy)
        to_sibling.setdefault((way, hop), []).append(copy)

    def ring_step(hop):
        ways = [way for way in range(2) if hop <= hops[way]]
        for way in ways:
            if hop < hops[way]:
                moving[way, hop + 1] = ring_copies(way, hop + 1)
                sent.extend(moving[way, hop + 1])
        for piece, (start, half) in enumerate(pieces):
            for way in ways:
                shard = at_ring(ring - signs[way] * hop)
                moving[way, hop][piece].wait_recv()
                if hop < hops[way]:
                    moving[way, hop + 1][piece].start()
                if piece < 2:
                    copy = remote(
                        block(shard, start, half),
                        block(shard, start, half),
                        part_s.at[way, hop, half],
                        part_r.at[way, hop, half],
                        {"dp": 1 - plane},
                    )
                    copy.start()
                    sent.append(copy)
                    across[way, hop, half] = copy
                sibling_copy(way, hop, piece, shard, start, half)

    def across_step(hop):
        for half in range(2):
            for way in range(2):
                if hop <= hops[way]:
                    shard = at_ring(ring - signs[way] * hop)
                    across[way, hop, half].wait_recv()
                    sibling_copy(way, hop, 4 + half, shard, other_third, half)

    square = (tokens_dev, tokens_dev)
    first = lax.broadcasted_iota(jnp.int32, square, 0)
    second = lax.broadcasted_iota(jnp.int32, square, 1)

    def ones_where(mask):
        return jnp.where(mask, 1.0, 0.0).astype(jnp.bfloat16)

    chosen = jnp.where(jnp.broadcast_to(row_ref[...], square) == first, 1.0, 0.0)
    to_cells = chosen.astype(jnp.bfloat16)
    to_slots = chosen.T.astype(jnp.bfloat16)
    same = ones_where(first == second)
    spot = first % CROSS
    shifts = (
        ones_where((second == first - 1) & (spot > 0)),
        ones_where((second == first + 1) & (spot < CROSS - 1)),
    )

    def times(left, right):
        return jnp.dot(left, right, preferred_element_type=jnp.float32)

    def clear(field):
        pad = jnp.zeros((CROSS, width), jnp.float32)
        for shift in range(3):
            for z in range(depth + 2):
                field[shift, z, 0] = pad
                field[shift, z, INLINE + 1] = pad

    def fill(field, layers, value):
        versions = (times(shifts[0], value), value.astype(jnp.float32), times(shifts[1], value))
        for shift in range(3):
            for at, z in enumerate(layers):
                field[shift, z, pl.ds(1, INLINE)] = versions[shift][
                    at * layer : (at + 1) * layer
                ].reshape(INLINE, CROSS, width)

    def halo_pair(which):
        up = remote(
            edge.at[which, 0],
            halo.at[which, 1],
            halo_s.at[which, 0],
            halo_r.at[which, 0],
            {"seq": (me + count - 1) % count},
        )
        down = remote(
            edge.at[which, 1],
            halo.at[which, 0],
            halo_s.at[which, 1],
            halo_r.at[which, 1],
            {"seq": (me + 1) % count},
        )
        return (up, down)

    def halo_start(which, value):
        edge[which, 0] = value[:layer]
        edge[which, 1] = value[tokens_dev - layer :]
        up, down = halo_pair(which)

        @pl.when(me > 0)
        def _():
            up.start()

        @pl.when(me < count - 1)
        def _():
            down.start()

    def halo_finish(which, field):
        up, down = halo_pair(which)

        @pl.when(me > 0)
        def _():
            down.wait_recv()
            up.wait_send()

        @pl.when(me < count - 1)
        def _():
            up.wait_recv()
            down.wait_send()

        fill(field, (0, depth + 1), halo[which].reshape(2 * layer, width))

    def window(field, z, i, c, lanes):
        return field[c, pl.ds(z, depth), pl.ds(i, INLINE), :, lanes]

    def lanes_of(j):
        return pl.ds(pl.multiple_of(j * LANES, LANES), LANES)

    def convolve(field, flip, start, stop):
        def body(j, carry):
            lanes = lanes_of(j)
            result = window(field, 1, 1, 1, lanes)
            for offset in range(27):
                z, i, c = (offset // 9, offset // 3 % 3, offset % 3)
                if flip:
                    z, i, c = (2 - z, 2 - i, 2 - c)
                result = result + ker_ref[pl.ds(offset, 1), lanes] * window(field, z, i, c, lanes)
            cells[:, lanes] = result.reshape(tokens_dev, LANES).astype(jnp.bfloat16)
            return carry

        lax.fori_loop(start, stop, body, 0)

    def kernel_sums():
        def body(j, carry):
            lanes = lanes_of(j)
            grad = window(field_d, 1, 1, 1, lanes)
            for offset in range(27):
                z, i, c = (offset // 9, offset // 3 % 3, offset % 3)
                product = grad * window(field_x, z, i, c, lanes)
                sums[pl.ds(offset, 1), lanes] = jnp.sum(
                    product.reshape(tokens_dev, LANES), axis=0, keepdims=True
                )
            return carry

        lax.fori_loop(0, width // LANES, body, 0)

    tile = 2 * LANES
    chunks = width // LANES
    own_layers = tuple(range(1, depth + 1))

    def turn_body(n, carry):
        at = pl.multiple_of(n * LANES, LANES)
        turned[pl.ds(at, LANES), :] = (
            dp_ref[:, pl.ds(at, LANES)].astype(jnp.float32).T.astype(jnp.bfloat16)
        )
        return carry

    def back_chip(position):
        at = pl.ds(pl.multiple_of(at_ring(position) // 2 * (2 * rows), 16), 2 * rows)
        back_rows[at, :] = times(w_all[at, :], turned[...]).astype(jnp.bfloat16)

    def back_step(hop):
        for way in range(2):
            for copy in to_sibling.get((way, hop), ()):
                copy.wait_recv()
        if hop <= min(hops):
            back_chip(ring - hop)
        if hop > 0:
            back_chip(ring + hop)

    lax.fori_loop(0, w_ref.shape[1] // LANES, turn_body, 0)
    clear(field_x)
    clear(field_d)
    ring_step(1)
    move_x = exchange(0, tok_ref)
    back_step(0)
    ring_step(2)
    across_step(1)
    grid_x = times(to_cells, landed(0, move_x)).astype(jnp.bfloat16)
    halo_start(0, grid_x)
    fill(field_x, own_layers, grid_x)
    for hop in range(3, line + 1):
        ring_step(hop)
        across_step(hop - 1)
        back_step(hop - 2)
    halo_finish(0, field_x)
    back_step(line - 1)
    across_step(line)
    back_step(line)

    move_d = outgoing(
        2,
        lax.dot_general(
            same,
            back_rows[...],
            (((1,), (1,)), ((), ())),
            preferred_element_type=jnp.float32,
        ),
    )
    convolve(field_x, False, 0, chunks)
    move_y = outgoing(1, times(to_slots, cells[...]))

    grid_d = times(to_cells, landed(2, move_d)).astype(jnp.bfloat16)
    halo_start(1, grid_d)
    fill(field_d, own_layers, grid_d)
    sums[pl.ds(3 * CROSS, CROSS)] = jnp.zeros((CROSS, width), jnp.float32)
    kernel_sums()

    def start_all(copies):
        for copy in copies:
            copy.start()
        sent.extend(copies)
        return copies

    def part_rows(core_at, plane_at):
        return pl.ds(pl.multiple_of((core_at * 2 + plane_at) * CROSS, CROSS), CROSS)

    home = part_rows(core, plane)
    squad = (
        (1 - core, plane, {"seq": sibling}),
        (core, 1 - plane, {"dp": 1 - plane}),
        (1 - core, 1 - plane, {"dp": 1 - plane, "seq": sibling}),
    )

    def scatter_sums():
        return start_all(
            [
                remote(
                    sums.at[part_rows(core_at, plane_at)],
                    arrived.at[k],
                    sum_s.at[0, k],
                    sum_r.at[0, k],
                    target,
                )
                for k, (core_at, plane_at, target) in enumerate(squad)
            ]
        )

    def pair_sums(copies):
        for copy in copies:
            copy.wait_recv()
        paired[...] = sums[home] + arrived[0] + arrived[1] + arrived[2]
        target = {"seq": me + 2 - 4 * chip_y}
        return start_all([remote(paired, arrived.at[3], sum_s.at[1, 0], sum_r.at[1, 0], target)])

    def line_sums(copies):
        for copy in copies:
            copy.wait_recv()
        layers[chip_z] = paired[...] + arrived[3]
        return start_all(
            [
                remote(
                    layers.at[chip_z],
                    layers.at[chip_z],
                    sum_s.at[2, k],
                    sum_r.at[2, k],
                    {"seq": (chip_z + k) % line * 4 + chip_y * 2 + core},
                )
                for k in range(1, line)
            ]
        )

    def share_sums(copies):
        for copy in copies:
            copy.wait_recv()
        whole_sum = layers[0]
        for k in range(1, line):
            whole_sum = whole_sum + layers[k]
        total[home] = whole_sum
        return start_all(
            [
                remote(total.at[home], total.at[home], sum_s.at[3, k], sum_r.at[3, k], target)
                for k, (core_at, plane_at, target) in enumerate(squad)
            ]
        )

    def finish_sums(copies):
        for copy in copies:
            copy.wait_recv()
        dker_ref[...] = total[: dker_ref.shape[0]]

    summing = scatter_sums()
    halo_finish(1, field_d)
    convolve(field_d, True, 0, chunks // 2)
    summing = pair_sums(summing)
    convolve(field_d, True, chunks // 2, chunks)
    summing = line_sums(summing)
    move_b = outgoing(3, times(to_slots, cells[...]))

    rows_y = landed(1, move_y)
    tiles = w_ref.shape[1] // tile

    def front_body(n, carry):
        at = pl.multiple_of(n * tile, tile)
        proj_ref[:, pl.ds(at, tile)] = times(rows_y, w_all[:, pl.ds(at, tile)]).astype(
            jnp.bfloat16
        )
        return carry

    lax.fori_loop(0, tiles // 2, front_body, 0)
    summing = share_sums(summing)
    lax.fori_loop(tiles // 2, tiles, front_body, 0)
    finish_sums(summing)
    dtok_ref[...] = landed(3, move_b)
    for copy in sent:
        copy.wait_send()


def copy_results(proj_in, dtok_in, dker_in, proj_out, dtok_out, dker_out):
    proj_out[...] = proj_in[...]
    dtok_out[...] = dtok_in[...]
    dker_out[...] = dker_in[...]


def fused_shards(tokens, place, kernel, proj_weight, d_projected):
    count = lax.axis_size("seq")
    tokens_dev, width = tokens.shape[1:]
    columns = proj_weight.shape[1]
    layer = INLINE * CROSS
    group = tokens_dev // count
    depth = tokens_dev // layer
    line = count // 4
    taps = kernel.shape[0]
    vmem = pl.BlockSpec(memory_space=pltpu.VMEM)
    dma = pltpu.SemaphoreType.DMA
    bf16, f32 = (jnp.bfloat16, jnp.float32)
    projected, d_tokens, d_kernel = pl.pallas_call(
        functools.partial(fused, count),
        out_shape=(
            jax.ShapeDtypeStruct((tokens_dev, columns), bf16),
            jax.ShapeDtypeStruct((tokens_dev, width), bf16),
            jax.ShapeDtypeStruct((taps, width), f32),
        ),
        in_specs=[vmem] * 5,
        out_specs=(vmem, vmem, vmem),
        scratch_shapes=[
            pltpu.VMEM((width, columns), bf16),
            pltpu.VMEM((4, count, group, width), bf16),
            pltpu.VMEM((4, count, group, width), bf16),
            pltpu.VMEM((2, 2, layer, width), bf16),
            pltpu.VMEM((2, 2, layer, width), bf16),
            pltpu.VMEM((3, depth + 2, INLINE + 2, CROSS, width), f32),
            pltpu.VMEM((3, depth + 2, INLINE + 2, CROSS, width), f32),
            pltpu.VMEM((tokens_dev, width), bf16),
            pltpu.VMEM((columns, tokens_dev), bf16),
            pltpu.VMEM((width, tokens_dev), bf16),
            pltpu.VMEM((4 * CROSS, width), f32),
            pltpu.VMEM((4, CROSS, width), f32),
            pltpu.VMEM((CROSS, width), f32),
            pltpu.VMEM((line, CROSS, width), f32),
            pltpu.VMEM((4 * CROSS, width), f32),
            dma((4, count)),
            dma((4, count)),
            dma((2, line + 1, 4)),
            dma((2, line + 1, 4)),
            dma((2, line + 1, 2)),
            dma((2, line + 1, 2)),
            dma((3, line + 1, 6)),
            dma((3, line + 1, 6)),
            dma((2, 2)),
            dma((2, 2)),
            dma((4, 4)),
            dma((4, 4)),
        ],
        compiler_params=pltpu.CompilerParams(
            collective_id=0, has_side_effects=True, vmem_limit_bytes=56 * 1024 * 1024
        ),
        cost_estimate=pl.CostEstimate(
            flops=4 * tokens_dev * width * columns,
            bytes_accessed=4 * tokens_dev * columns,
            transcendentals=0,
        ),
    )(
        tokens[0].reshape(count, group, width),
        place,
        kernel,
        proj_weight,
        d_projected[0],
    )
    results = [projected, d_tokens, d_kernel]
    projected, d_tokens, d_kernel = pl.pallas_call(
        copy_results,
        out_shape=tuple(jax.ShapeDtypeStruct(r.shape, r.dtype) for r in results),
        in_specs=[vmem] * 3,
        out_specs=(vmem,) * 3,
    )(*results)
    return (projected[None], d_tokens[None], d_kernel)


def solution(mesh):
    placed = (P("dp", "seq", None), P("seq", None), P(), P("seq", None), P("dp", "seq", None))
    count = mesh.shape["seq"]
    use_kernel = mesh.shape["dp"] == 2 and count == 16
    return jax.shard_map(
        fused_shards if use_kernel else shards,
        mesh=mesh,
        in_specs=placed,
        out_specs=(P("dp", "seq", None), P("dp", "seq", None), P()),
        check_vma=False,
    )
```

```python
import functools

import jax
import jax.numpy as jnp
from jax import lax
from jax.experimental import pallas as pl
from jax.experimental.pallas import tpu as pltpu
from jax.sharding import PartitionSpec as P

INLINE = 8
CROSS = 8
MESH = pl.DeviceIdType.MESH
LANES = 128


def with_halo(value, sides, width):
    for axis, dim in sides:
        size, length = (lax.axis_size(axis), value.shape[dim])
        up = [(i, (i + 1) % size) for i in range(size - 1)]
        down = [(j, i) for i, j in up]
        last = lax.slice_in_dim(value, length - width, length, axis=dim)
        first = lax.slice_in_dim(value, 0, width, axis=dim)
        before = lax.ppermute(last, axis, up)
        after = lax.ppermute(first, axis, down)
        value = jnp.concatenate([before, value, after], axis=dim)
    return value


def brick_cells(landed, inverse):
    tokens_dev = inverse.shape[0]
    width = landed.shape[-1]
    slots = landed.reshape(tokens_dev, width)
    cells = jnp.take(slots, inverse, axis=0)
    return cells.reshape(tokens_dev // (INLINE * CROSS), INLINE, CROSS, width)


def scan_pieces(cells, order, count):
    width = cells.shape[-1]
    tokens_dev = order.shape[0]
    slots = jnp.take(cells.reshape(tokens_dev, width), order, axis=0)
    return slots.reshape(count, tokens_dev // count, width)


def to_bricks(rows, inverse, count):
    tokens_dev, width = rows.shape
    landed = lax.all_to_all(
        rows.reshape(count, tokens_dev // count, width),
        "seq",
        split_axis=0,
        concat_axis=0,
        tiled=True,
    )
    return brick_cells(landed, inverse)


def to_scan(cells, order, count):
    landed = lax.all_to_all(
        scan_pieces(cells, order, count), "seq", split_axis=0, concat_axis=0, tiled=True
    )
    return landed.reshape(order.shape[0], cells.shape[-1])


def with_faces(block):
    deeper = with_halo(block, (("seq", 0),), 1)
    return jnp.pad(deeper, ((0, 0), (1, 1), (1, 1), (0, 0)))


def window(field, depth_dev, start_z, start_i, start_c):
    return field[
        start_z : start_z + depth_dev, start_i : start_i + INLINE, start_c : start_c + CROSS
    ].astype(jnp.float32)


def forward_conv(grid_x, pad_x, kernel, depth_dev):
    conv = jnp.zeros(grid_x.shape, jnp.float32)
    for offset in range(27):
        conv = conv + kernel[offset] * window(
            pad_x, depth_dev, offset // 9, offset // 3 % 3, offset % 3
        )
    return (grid_x.astype(jnp.float32) + conv).astype(jnp.bfloat16)


def backward_conv(grid_d, pad_d, pad_x, kernel, depth_dev):
    grid_float = grid_d.astype(jnp.float32)
    back = grid_float
    partial_value = []
    for offset in range(27):
        dz, di, dc = (offset // 9, offset // 3 % 3, offset % 3)
        back = back + kernel[offset] * window(pad_d, depth_dev, 2 - dz, 2 - di, 2 - dc)
        partial_value.append(
            jnp.sum(grid_float * window(pad_x, depth_dev, dz, di, dc), axis=(0, 1, 2))
        )
    return (back.astype(jnp.bfloat16), jnp.stack(partial_value))


def shards(tokens, place, kernel, proj_weight, d_projected):
    count = lax.axis_size("seq")
    order = place[0]
    inverse = jnp.argsort(order)
    rows_x = tokens[0]
    d_rows = d_projected[0]
    depth_dev = rows_x.shape[0] // (INLINE * CROSS)
    d_y = lax.dot_general(
        d_rows,
        lax.all_gather(proj_weight, "seq", axis=0, tiled=True),
        (((1,), (1,)), ((), ())),
        preferred_element_type=jnp.float32,
    )
    d_y = d_y.astype(jnp.bfloat16)
    grid_x = to_bricks(rows_x, inverse, count)
    pad_x = with_faces(grid_x)
    grid_y = forward_conv(grid_x, pad_x, kernel, depth_dev)
    rows_y = to_scan(grid_y, order, count)
    grid_d = to_bricks(d_y, inverse, count)
    pad_d = with_faces(grid_d)
    back, partial_value = backward_conv(grid_d, pad_d, pad_x, kernel, depth_dev)
    d_tokens = to_scan(back, order, count)
    projected = jnp.dot(
        rows_y,
        lax.all_gather(proj_weight, "seq", axis=0, tiled=True),
        preferred_element_type=jnp.float32,
    )
    projected = projected.astype(jnp.bfloat16)
    d_kernel = lax.psum(partial_value, ("dp", "seq"))
    return (projected[None], d_tokens[None], d_kernel)


def fused(
    count,
    tok_ref,
    row_ref,
    ker_ref,
    w_ref,
    dp_ref,
    proj_ref,
    dtok_ref,
    dker_ref,
    w_all,
    land,
    send,
    edge,
    halo,
    field_x,
    field_d,
    cells,
    turned,
    back_rows,
    sums,
    arrived,
    paired,
    layers,
    total,
    move_s,
    move_r,
    ring_s,
    ring_r,
    part_s,
    part_r,
    sib_s,
    sib_r,
    halo_s,
    halo_r,
    sum_s,
    sum_r,
):
    me = lax.axis_index("seq")
    plane = lax.axis_index("dp")
    tokens_dev, width = cells.shape
    rows = w_ref.shape[0]
    third = w_ref.shape[1] // 3
    layer = INLINE * CROSS
    depth = tokens_dev // layer
    group = tokens_dev // count
    chips = count // 2
    line = chips // 2
    core = me % 2
    chip = me // 2
    chip_y = chip % 2
    chip_z = chip // 2
    ring = chip_z * (1 - chip_y) + (chips - 1 - chip_z) * chip_y
    sibling = me + 1 - 2 * core
    sign = 1 - 2 * core
    own_third = pl.multiple_of((1 + plane) * third, LANES)
    other_third = pl.multiple_of((2 - plane) * third, LANES)

    def at_ring(position):
        spot = (position + 2 * chips) % chips
        side = spot // line
        z = spot * (1 - side) + (chips - 1 - spot) * side
        return (z * 2 + side) * 2 + core

    upper = (rows // 32 + rows // 16 % 2) * 16
    halves = ((0, upper), (upper, rows - upper))

    def block(shard, start, half):
        low, size = halves[half]
        return w_all.at[pl.ds(pl.multiple_of(shard * rows + low, 16), size), pl.ds(start, third)]

    def whole(shard):
        return w_all.at[pl.ds(pl.multiple_of(shard * rows, 16), rows), :]

    def remote(src, dst, s_sem, r_sem, target):
        return pltpu.make_async_remote_copy(
            src_ref=src,
            dst_ref=dst,
            send_sem=s_sem,
            recv_sem=r_sem,
            device_id=target,
            device_id_type=MESH,
        )

    edge_zero = jnp.zeros((layer, width), jnp.bfloat16)
    for which in range(2):
        for side in range(2):
            halo[which, side] = edge_zero
    w_all[pl.ds(pl.multiple_of(me * rows, 16), rows), :] = w_ref[...]

    barrier = pltpu.get_barrier_semaphore()
    for step in range(1, count):
        pl.semaphore_signal(
            barrier, inc=1, device_id={"seq": (me + step) % count}, device_id_type=MESH
        )
    pl.semaphore_signal(barrier, inc=1, device_id={"dp": 1 - plane}, device_id_type=MESH)
    pl.semaphore_signal(
        barrier, inc=1, device_id={"dp": 1 - plane, "seq": sibling}, device_id_type=MESH
    )
    pl.semaphore_wait(barrier, count + 1)

    sent = []

    def exchange(which, source, lanes=None, row=None):
        lanes = pl.ds(0, width) if lanes is None else lanes
        row = which if row is None else row
        copies = []
        for step in range(1, count):
            target = (me + step) % count
            copies.append(
                remote(
                    source.at[target, :, lanes],
                    land.at[which, me, :, lanes],
                    move_s.at[row, step],
                    move_r.at[row, step],
                    {"seq": target},
                )
            )
        for copy in copies:
            copy.start()
        sent.extend(copies)
        land[which, pl.ds(me, 1), :, lanes] = source[pl.ds(me, 1), :, lanes]
        return copies

    def landed(which, copies):
        for copy in copies:
            copy.wait_recv()
        value = land[which].astype(jnp.float32)
        return value.reshape(tokens_dev, width).astype(jnp.bfloat16)

    def outgoing(which, slots):
        send[which] = slots.reshape(count, group, width).astype(jnp.bfloat16)
        return exchange(which, send.at[which])

    hops = (line, chips - 1 - line)
    pieces = ((own_third, 0), (own_third, 1), (0, 0), (0, 1))
    signs = (sign, -sign)

    def ring_copies(way, hop):
        shard = at_ring(ring - signs[way] * (hop - 1))
        target = {"seq": at_ring(ring + signs[way])}
        pair = []
        for piece, (start, half) in enumerate(pieces):
            pair.append(
                remote(
                    block(shard, start, half),
                    block(shard, start, half),
                    ring_s.at[way, hop, piece],
                    ring_r.at[way, hop, piece],
                    target,
                )
            )
        return pair

    moving = {}
    for way in range(2):
        moving[way, 1] = ring_copies(way, 1)
    for piece in range(len(pieces)):
        for way in range(2):
            moving[way, 1][piece].start()
    for way in range(2):
        sent.extend(moving[way, 1])
    own_copy = remote(
        whole(me), whole(me), sib_s.at[0, 0, 0], sib_r.at[0, 0, 0], {"seq": sibling}
    )
    own_copy.start()
    sent.append(own_copy)
    to_sibling = {(0, 0): [own_copy]}
    across = {}

    def sibling_copy(way, hop, piece, shard, start, half):
        copy = remote(
            block(shard, start, half),
            block(shard, start, half),
            sib_s.at[1 + way, hop, piece],
            sib_r.at[1 + way, hop, piece],
            {"seq": sibling},
        )
        copy.start()
        sent.append(copy)
        to_sibling.setdefault((way, hop), []).append(copy)

    def ring_step(hop):
        ways = [way for way in range(2) if hop <= hops[way]]
        for way in ways:
            if hop < hops[way]:
                moving[way, hop + 1] = ring_copies(way, hop + 1)
                sent.extend(moving[way, hop + 1])
        for piece, (start, half) in enumerate(pieces):
            for way in ways:
                shard = at_ring(ring - signs[way] * hop)
                moving[way, hop][piece].wait_recv()
                if hop < hops[way]:
                    moving[way, hop + 1][piece].start()
                if piece < 2:
                    copy = remote(
                        block(shard, start, half),
                        block(shard, start, half),
                        part_s.at[way, hop, half],
                        part_r.at[way, hop, half],
                        {"dp": 1 - plane},
                    )
                    copy.start()
                    sent.append(copy)
                    across[way, hop, half] = copy
                sibling_copy(way, hop, piece, shard, start, half)

    def across_step(hop):
        for half in range(2):
            for way in range(2):
                if hop <= hops[way]:
                    shard = at_ring(ring - signs[way] * hop)
                    across[way, hop, half].wait_recv()
                    sibling_copy(way, hop, 4 + half, shard, other_third, half)

    square = (tokens_dev, tokens_dev)
    first = lax.broadcasted_iota(jnp.int32, square, 0)
    second = lax.broadcasted_iota(jnp.int32, square, 1)

    def ones_where(mask):
        return jnp.where(mask, 1.0, 0.0).astype(jnp.bfloat16)

    chosen = jnp.where(jnp.broadcast_to(row_ref[...], square) == first, 1.0, 0.0)
    to_cells = chosen.astype(jnp.bfloat16)
    to_slots = chosen.T.astype(jnp.bfloat16)
    same = ones_where(first == second)
    spot = first % CROSS
    shifts = (
        ones_where((second == first - 1) & (spot > 0)),
        ones_where((second == first + 1) & (spot < CROSS - 1)),
    )

    def times(left, right):
        return jnp.dot(left, right, preferred_element_type=jnp.float32)

    def clear(field):
        pad = jnp.zeros((CROSS, width), jnp.float32)
        for shift in range(3):
            for z in range(depth + 2):
                field[shift, z, 0] = pad
                field[shift, z, INLINE + 1] = pad

    def fill(field, layers, value):
        versions = (times(shifts[0], value), value.astype(jnp.float32), times(shifts[1], value))
        for shift in range(3):
            for at, z in enumerate(layers):
                field[shift, z, pl.ds(1, INLINE)] = versions[shift][
                    at * layer : (at + 1) * layer
                ].reshape(INLINE, CROSS, width)

    def halo_pair(which):
        up = remote(
            edge.at[which, 0],
            halo.at[which, 1],
            halo_s.at[which, 0],
            halo_r.at[which, 0],
            {"seq": (me + count - 1) % count},
        )
        down = remote(
            edge.at[which, 1],
            halo.at[which, 0],
            halo_s.at[which, 1],
            halo_r.at[which, 1],
            {"seq": (me + 1) % count},
        )
        return (up, down)

    def halo_start(which, value):
        edge[which, 0] = value[:layer]
        edge[which, 1] = value[tokens_dev - layer :]
        up, down = halo_pair(which)

        @pl.when(me > 0)
        def _():
            up.start()

        @pl.when(me < count - 1)
        def _():
            down.start()

    def halo_finish(which, field):
        up, down = halo_pair(which)

        @pl.when(me > 0)
        def _():
            down.wait_recv()
            up.wait_send()

        @pl.when(me < count - 1)
        def _():
            up.wait_recv()
            down.wait_send()

        fill(field, (0, depth + 1), halo[which].reshape(2 * layer, width))

    def window(field, z, i, c, lanes):
        return field[c, pl.ds(z, depth), pl.ds(i, INLINE), :, lanes]

    def lanes_of(j):
        return pl.ds(pl.multiple_of(j * LANES, LANES), LANES)

    def convolve(field, flip, start, stop):
        def body(j, carry):
            lanes = lanes_of(j)
            result = window(field, 1, 1, 1, lanes)
            for offset in range(27):
                z, i, c = (offset // 9, offset // 3 % 3, offset % 3)
                if flip:
                    z, i, c = (2 - z, 2 - i, 2 - c)
                result = result + ker_ref[pl.ds(offset, 1), lanes] * window(field, z, i, c, lanes)
            cells[:, lanes] = result.reshape(tokens_dev, LANES).astype(jnp.bfloat16)
            return carry

        lax.fori_loop(start, stop, body, 0)

    def kernel_sums():
        def body(j, carry):
            lanes = lanes_of(j)
            grad = window(field_d, 1, 1, 1, lanes)
            for offset in range(27):
                z, i, c = (offset // 9, offset // 3 % 3, offset % 3)
                product = grad * window(field_x, z, i, c, lanes)
                sums[pl.ds(offset, 1), lanes] = jnp.sum(
                    product.reshape(tokens_dev, LANES), axis=0, keepdims=True
                )
            return carry

        lax.fori_loop(0, width // LANES, body, 0)

    tile = 2 * LANES
    chunks = width // LANES
    own_layers = tuple(range(1, depth + 1))

    def turn_body(n, carry):
        at = pl.multiple_of(n * LANES, LANES)
        turned[pl.ds(at, LANES), :] = (
            dp_ref[:, pl.ds(at, LANES)].astype(jnp.float32).T.astype(jnp.bfloat16)
        )
        return carry

    def back_chip(position):
        at = pl.ds(pl.multiple_of(at_ring(position) // 2 * (2 * rows), 16), 2 * rows)
        back_rows[at, :] = times(w_all[at, :], turned[...]).astype(jnp.bfloat16)

    def back_step(hop):
        for way in range(2):
            for copy in to_sibling.get((way, hop), ()):
                copy.wait_recv()
        if hop <= min(hops):
            back_chip(ring - hop)
        if hop > 0:
            back_chip(ring + hop)

    lax.fori_loop(0, w_ref.shape[1] // LANES, turn_body, 0)
    clear(field_x)
    clear(field_d)
    ring_step(1)
    move_x = exchange(0, tok_ref)
    back_step(0)
    ring_step(2)
    across_step(1)
    grid_x = times(to_cells, landed(0, move_x)).astype(jnp.bfloat16)
    halo_start(0, grid_x)
    fill(field_x, own_layers, grid_x)
    for hop in range(3, line + 1):
        ring_step(hop)
        across_step(hop - 1)
        back_step(hop - 2)
    halo_finish(0, field_x)
    back_step(line - 1)
    across_step(line)
    back_step(line)

    move_d = outgoing(
        2,
        lax.dot_general(
            same,
            back_rows[...],
            (((1,), (1,)), ((), ())),
            preferred_element_type=jnp.float32,
        ),
    )
    convolve(field_x, False, 0, chunks)
    move_y = outgoing(1, times(to_slots, cells[...]))

    grid_d = times(to_cells, landed(2, move_d)).astype(jnp.bfloat16)
    halo_start(1, grid_d)
    fill(field_d, own_layers, grid_d)
    sums[pl.ds(3 * CROSS, CROSS)] = jnp.zeros((CROSS, width), jnp.float32)
    kernel_sums()

    def start_all(copies):
        for copy in copies:
            copy.start()
        sent.extend(copies)
        return copies

    def part_rows(core_at, plane_at):
        return pl.ds(pl.multiple_of((core_at * 2 + plane_at) * CROSS, CROSS), CROSS)

    home = part_rows(core, plane)
    squad = (
        (1 - core, plane, {"seq": sibling}),
        (core, 1 - plane, {"dp": 1 - plane}),
        (1 - core, 1 - plane, {"dp": 1 - plane, "seq": sibling}),
    )

    def scatter_sums():
        return start_all(
            [
                remote(
                    sums.at[part_rows(core_at, plane_at)],
                    arrived.at[k],
                    sum_s.at[0, k],
                    sum_r.at[0, k],
                    target,
                )
                for k, (core_at, plane_at, target) in enumerate(squad)
            ]
        )

    def pair_sums(copies):
        for copy in copies:
            copy.wait_recv()
        paired[...] = sums[home] + arrived[0] + arrived[1] + arrived[2]
        target = {"seq": me + 2 - 4 * chip_y}
        return start_all([remote(paired, arrived.at[3], sum_s.at[1, 0], sum_r.at[1, 0], target)])

    def line_sums(copies):
        for copy in copies:
            copy.wait_recv()
        layers[chip_z] = paired[...] + arrived[3]
        return start_all(
            [
                remote(
                    layers.at[chip_z],
                    layers.at[chip_z],
                    sum_s.at[2, k],
                    sum_r.at[2, k],
                    {"seq": (chip_z + k) % line * 4 + chip_y * 2 + core},
                )
                for k in range(1, line)
            ]
        )

    def share_sums(copies):
        for copy in copies:
            copy.wait_recv()
        whole_sum = layers[0]
        for k in range(1, line):
            whole_sum = whole_sum + layers[k]
        total[home] = whole_sum
        return start_all(
            [
                remote(total.at[home], total.at[home], sum_s.at[3, k], sum_r.at[3, k], target)
                for k, (core_at, plane_at, target) in enumerate(squad)
            ]
        )

    def finish_sums(copies):
        for copy in copies:
            copy.wait_recv()
        dker_ref[...] = total[: dker_ref.shape[0]]

    summing = scatter_sums()
    halo_finish(1, field_d)
    middle = chunks // 2 * LANES

    def send_half(row, low, size):
        lanes = pl.ds(low, size)
        slots = times(to_slots, cells[:, lanes])
        send[3, :, :, lanes] = slots.reshape(count, group, size).astype(jnp.bfloat16)
        return exchange(3, send.at[3], lanes, row)

    convolve(field_d, True, 0, chunks // 2)
    summing = pair_sums(summing)
    move_b = send_half(3, 0, middle)
    convolve(field_d, True, chunks // 2, chunks)
    summing = line_sums(summing)
    move_b = move_b + send_half(4, middle, width - middle)

    rows_y = landed(1, move_y)
    tiles = w_ref.shape[1] // tile

    def front_body(n, carry):
        at = pl.multiple_of(n * tile, tile)
        proj_ref[:, pl.ds(at, tile)] = times(rows_y, w_all[:, pl.ds(at, tile)]).astype(
            jnp.bfloat16
        )
        return carry

    lax.fori_loop(0, tiles // 2, front_body, 0)
    summing = share_sums(summing)
    lax.fori_loop(tiles // 2, tiles, front_body, 0)
    finish_sums(summing)
    dtok_ref[...] = landed(3, move_b)
    for copy in sent:
        copy.wait_send()


def copy_results(proj_in, dtok_in, dker_in, proj_out, dtok_out, dker_out):
    proj_out[...] = proj_in[...]
    dtok_out[...] = dtok_in[...]
    dker_out[...] = dker_in[...]


def fused_shards(tokens, place, kernel, proj_weight, d_projected):
    count = lax.axis_size("seq")
    tokens_dev, width = tokens.shape[1:]
    columns = proj_weight.shape[1]
    layer = INLINE * CROSS
    group = tokens_dev // count
    depth = tokens_dev // layer
    line = count // 4
    taps = kernel.shape[0]
    vmem = pl.BlockSpec(memory_space=pltpu.VMEM)
    dma = pltpu.SemaphoreType.DMA
    bf16, f32 = (jnp.bfloat16, jnp.float32)
    projected, d_tokens, d_kernel = pl.pallas_call(
        functools.partial(fused, count),
        out_shape=(
            jax.ShapeDtypeStruct((tokens_dev, columns), bf16),
            jax.ShapeDtypeStruct((tokens_dev, width), bf16),
            jax.ShapeDtypeStruct((taps, width), f32),
        ),
        in_specs=[vmem] * 5,
        out_specs=(vmem, vmem, vmem),
        scratch_shapes=[
            pltpu.VMEM((width, columns), bf16),
            pltpu.VMEM((4, count, group, width), bf16),
            pltpu.VMEM((4, count, group, width), bf16),
            pltpu.VMEM((2, 2, layer, width), bf16),
            pltpu.VMEM((2, 2, layer, width), bf16),
            pltpu.VMEM((3, depth + 2, INLINE + 2, CROSS, width), f32),
            pltpu.VMEM((3, depth + 2, INLINE + 2, CROSS, width), f32),
            pltpu.VMEM((tokens_dev, width), bf16),
            pltpu.VMEM((columns, tokens_dev), bf16),
            pltpu.VMEM((width, tokens_dev), bf16),
            pltpu.VMEM((4 * CROSS, width), f32),
            pltpu.VMEM((4, CROSS, width), f32),
            pltpu.VMEM((CROSS, width), f32),
            pltpu.VMEM((line, CROSS, width), f32),
            pltpu.VMEM((4 * CROSS, width), f32),
            dma((5, count)),
            dma((5, count)),
            dma((2, line + 1, 4)),
            dma((2, line + 1, 4)),
            dma((2, line + 1, 2)),
            dma((2, line + 1, 2)),
            dma((3, line + 1, 6)),
            dma((3, line + 1, 6)),
            dma((2, 2)),
            dma((2, 2)),
            dma((4, 4)),
            dma((4, 4)),
        ],
        compiler_params=pltpu.CompilerParams(
            collective_id=0, has_side_effects=True, vmem_limit_bytes=56 * 1024 * 1024
        ),
        cost_estimate=pl.CostEstimate(
            flops=4 * tokens_dev * width * columns,
            bytes_accessed=4 * tokens_dev * columns,
            transcendentals=0,
        ),
    )(
        tokens[0].reshape(count, group, width),
        place,
        kernel,
        proj_weight,
        d_projected[0],
    )
    results = [projected, d_tokens, d_kernel]
    projected, d_tokens, d_kernel = pl.pallas_call(
        copy_results,
        out_shape=tuple(jax.ShapeDtypeStruct(r.shape, r.dtype) for r in results),
        in_specs=[vmem] * 3,
        out_specs=(vmem,) * 3,
    )(*results)
    return (projected[None], d_tokens[None], d_kernel)


def solution(mesh):
    placed = (P("dp", "seq", None), P("seq", None), P(), P("seq", None), P("dp", "seq", None))
    count = mesh.shape["seq"]
    use_kernel = mesh.shape["dp"] == 2 and count == 16
    return jax.shard_map(
        fused_shards if use_kernel else shards,
        mesh=mesh,
        in_specs=placed,
        out_specs=(P("dp", "seq", None), P("dp", "seq", None), P()),
        check_vma=False,
    )
```

```python
import functools

import jax
import jax.numpy as jnp
from jax import lax
from jax.experimental import pallas as pl
from jax.experimental.pallas import tpu as pltpu
from jax.sharding import PartitionSpec as P

INLINE = 8
CROSS = 8
MESH = pl.DeviceIdType.MESH
LANES = 128


def with_halo(value, sides, width):
    for axis, dim in sides:
        size, length = (lax.axis_size(axis), value.shape[dim])
        up = [(i, (i + 1) % size) for i in range(size - 1)]
        down = [(j, i) for i, j in up]
        last = lax.slice_in_dim(value, length - width, length, axis=dim)
        first = lax.slice_in_dim(value, 0, width, axis=dim)
        before = lax.ppermute(last, axis, up)
        after = lax.ppermute(first, axis, down)
        value = jnp.concatenate([before, value, after], axis=dim)
    return value


def brick_cells(landed, inverse):
    tokens_dev = inverse.shape[0]
    width = landed.shape[-1]
    slots = landed.reshape(tokens_dev, width)
    cells = jnp.take(slots, inverse, axis=0)
    return cells.reshape(tokens_dev // (INLINE * CROSS), INLINE, CROSS, width)


def scan_pieces(cells, order, count):
    width = cells.shape[-1]
    tokens_dev = order.shape[0]
    slots = jnp.take(cells.reshape(tokens_dev, width), order, axis=0)
    return slots.reshape(count, tokens_dev // count, width)


def to_bricks(rows, inverse, count):
    tokens_dev, width = rows.shape
    landed = lax.all_to_all(
        rows.reshape(count, tokens_dev // count, width),
        "seq",
        split_axis=0,
        concat_axis=0,
        tiled=True,
    )
    return brick_cells(landed, inverse)


def to_scan(cells, order, count):
    landed = lax.all_to_all(
        scan_pieces(cells, order, count), "seq", split_axis=0, concat_axis=0, tiled=True
    )
    return landed.reshape(order.shape[0], cells.shape[-1])


def with_faces(block):
    deeper = with_halo(block, (("seq", 0),), 1)
    return jnp.pad(deeper, ((0, 0), (1, 1), (1, 1), (0, 0)))


def window(field, depth_dev, start_z, start_i, start_c):
    return field[
        start_z : start_z + depth_dev, start_i : start_i + INLINE, start_c : start_c + CROSS
    ].astype(jnp.float32)


def forward_conv(grid_x, pad_x, kernel, depth_dev):
    conv = jnp.zeros(grid_x.shape, jnp.float32)
    for offset in range(27):
        conv = conv + kernel[offset] * window(
            pad_x, depth_dev, offset // 9, offset // 3 % 3, offset % 3
        )
    return (grid_x.astype(jnp.float32) + conv).astype(jnp.bfloat16)


def backward_conv(grid_d, pad_d, pad_x, kernel, depth_dev):
    grid_float = grid_d.astype(jnp.float32)
    back = grid_float
    partial_value = []
    for offset in range(27):
        dz, di, dc = (offset // 9, offset // 3 % 3, offset % 3)
        back = back + kernel[offset] * window(pad_d, depth_dev, 2 - dz, 2 - di, 2 - dc)
        partial_value.append(
            jnp.sum(grid_float * window(pad_x, depth_dev, dz, di, dc), axis=(0, 1, 2))
        )
    return (back.astype(jnp.bfloat16), jnp.stack(partial_value))


def shards(tokens, place, kernel, proj_weight, d_projected):
    count = lax.axis_size("seq")
    order = place[0]
    inverse = jnp.argsort(order)
    rows_x = tokens[0]
    d_rows = d_projected[0]
    depth_dev = rows_x.shape[0] // (INLINE * CROSS)
    d_y = lax.dot_general(
        d_rows,
        lax.all_gather(proj_weight, "seq", axis=0, tiled=True),
        (((1,), (1,)), ((), ())),
        preferred_element_type=jnp.float32,
    )
    d_y = d_y.astype(jnp.bfloat16)
    grid_x = to_bricks(rows_x, inverse, count)
    pad_x = with_faces(grid_x)
    grid_y = forward_conv(grid_x, pad_x, kernel, depth_dev)
    rows_y = to_scan(grid_y, order, count)
    grid_d = to_bricks(d_y, inverse, count)
    pad_d = with_faces(grid_d)
    back, partial_value = backward_conv(grid_d, pad_d, pad_x, kernel, depth_dev)
    d_tokens = to_scan(back, order, count)
    projected = jnp.dot(
        rows_y,
        lax.all_gather(proj_weight, "seq", axis=0, tiled=True),
        preferred_element_type=jnp.float32,
    )
    projected = projected.astype(jnp.bfloat16)
    d_kernel = lax.psum(partial_value, ("dp", "seq"))
    return (projected[None], d_tokens[None], d_kernel)


def fused(
    count,
    tok_ref,
    row_ref,
    ker_ref,
    w_ref,
    dp_ref,
    proj_ref,
    dtok_ref,
    dker_ref,
    w_all,
    land,
    send,
    edge,
    halo,
    field_x,
    field_d,
    cells,
    turned,
    back_rows,
    sums,
    arrived,
    paired,
    layers,
    total,
    move_s,
    move_r,
    ring_s,
    ring_r,
    part_s,
    part_r,
    sib_s,
    sib_r,
    halo_s,
    halo_r,
    sum_s,
    sum_r,
):
    me = lax.axis_index("seq")
    plane = lax.axis_index("dp")
    tokens_dev, width = cells.shape
    rows = w_ref.shape[0]
    third = w_ref.shape[1] // 3
    layer = INLINE * CROSS
    depth = tokens_dev // layer
    group = tokens_dev // count
    chips = count // 2
    line = chips // 2
    core = me % 2
    chip = me // 2
    chip_y = chip % 2
    chip_z = chip // 2
    ring = chip_z * (1 - chip_y) + (chips - 1 - chip_z) * chip_y
    sibling = me + 1 - 2 * core
    sign = 1 - 2 * core
    own_third = pl.multiple_of((1 + plane) * third, LANES)
    other_third = pl.multiple_of((2 - plane) * third, LANES)

    def at_ring(position):
        spot = (position + 2 * chips) % chips
        side = spot // line
        z = spot * (1 - side) + (chips - 1 - spot) * side
        return (z * 2 + side) * 2 + core

    upper = (rows // 32 + rows // 16 % 2) * 16
    halves = ((0, upper), (upper, rows - upper))

    def block(shard, start, half):
        low, size = halves[half]
        return w_all.at[pl.ds(pl.multiple_of(shard * rows + low, 16), size), pl.ds(start, third)]

    def whole(shard):
        return w_all.at[pl.ds(pl.multiple_of(shard * rows, 16), rows), :]

    def remote(src, dst, s_sem, r_sem, target):
        return pltpu.make_async_remote_copy(
            src_ref=src,
            dst_ref=dst,
            send_sem=s_sem,
            recv_sem=r_sem,
            device_id=target,
            device_id_type=MESH,
        )

    edge_zero = jnp.zeros((layer, width), jnp.bfloat16)
    for which in range(2):
        for side in range(2):
            halo[which, side] = edge_zero
    w_all[pl.ds(pl.multiple_of(me * rows, 16), rows), :] = w_ref[...]

    barrier = pltpu.get_barrier_semaphore()
    for step in range(1, count):
        pl.semaphore_signal(
            barrier, inc=1, device_id={"seq": (me + step) % count}, device_id_type=MESH
        )
    pl.semaphore_signal(barrier, inc=1, device_id={"dp": 1 - plane}, device_id_type=MESH)
    pl.semaphore_signal(
        barrier, inc=1, device_id={"dp": 1 - plane, "seq": sibling}, device_id_type=MESH
    )
    pl.semaphore_wait(barrier, count + 1)

    sent = []

    def exchange(which, source):
        copies = []
        for step in range(1, count):
            target = (me + step) % count
            copies.append(
                remote(
                    source.at[target],
                    land.at[which, me],
                    move_s.at[which, step],
                    move_r.at[which, step],
                    {"seq": target},
                )
            )
        for copy in copies:
            copy.start()
        sent.extend(copies)
        land[which, pl.ds(me, 1)] = source[pl.ds(me, 1)]
        return copies

    def landed(which, copies):
        for copy in copies:
            copy.wait_recv()
        value = land[which].astype(jnp.float32)
        return value.reshape(tokens_dev, width).astype(jnp.bfloat16)

    def outgoing(which, slots):
        send[which] = slots.reshape(count, group, width).astype(jnp.bfloat16)
        return exchange(which, send.at[which])

    hops = (line, chips - 1 - line)
    pieces = ((own_third, 0), (own_third, 1), (0, 0), (0, 1))
    signs = (sign, -sign)

    def ring_copies(way, hop):
        shard = at_ring(ring - signs[way] * (hop - 1))
        target = {"seq": at_ring(ring + signs[way])}
        pair = []
        for piece, (start, half) in enumerate(pieces):
            pair.append(
                remote(
                    block(shard, start, half),
                    block(shard, start, half),
                    ring_s.at[way, hop, piece],
                    ring_r.at[way, hop, piece],
                    target,
                )
            )
        return pair

    moving = {}
    for way in range(2):
        moving[way, 1] = ring_copies(way, 1)
    for piece in range(len(pieces)):
        for way in range(2):
            moving[way, 1][piece].start()
    for way in range(2):
        sent.extend(moving[way, 1])
    own_copy = remote(
        whole(me), whole(me), sib_s.at[0, 0, 0], sib_r.at[0, 0, 0], {"seq": sibling}
    )
    own_copy.start()
    sent.append(own_copy)
    to_sibling = {(0, 0): [own_copy]}
    across = {}

    def sibling_copy(way, hop, piece, shard, start, half):
        copy = remote(
            block(shard, start, half),
            block(shard, start, half),
            sib_s.at[1 + way, hop, piece],
            sib_r.at[1 + way, hop, piece],
            {"seq": sibling},
        )
        copy.start()
        sent.append(copy)
        to_sibling.setdefault((way, hop), []).append(copy)

    def ring_step(hop):
        ways = [way for way in range(2) if hop <= hops[way]]
        for way in ways:
            if hop < hops[way]:
                moving[way, hop + 1] = ring_copies(way, hop + 1)
                sent.extend(moving[way, hop + 1])
        for piece, (start, half) in enumerate(pieces):
            for way in ways:
                shard = at_ring(ring - signs[way] * hop)
                moving[way, hop][piece].wait_recv()
                if hop < hops[way]:
                    moving[way, hop + 1][piece].start()
                if piece < 2:
                    copy = remote(
                        block(shard, start, half),
                        block(shard, start, half),
                        part_s.at[way, hop, half],
                        part_r.at[way, hop, half],
                        {"dp": 1 - plane},
                    )
                    copy.start()
                    sent.append(copy)
                    across[way, hop, half] = copy
                sibling_copy(way, hop, piece, shard, start, half)

    def across_step(hop):
        for half in range(2):
            for way in range(2):
                if hop <= hops[way]:
                    shard = at_ring(ring - signs[way] * hop)
                    across[way, hop, half].wait_recv()
                    sibling_copy(way, hop, 4 + half, shard, other_third, half)

    square = (tokens_dev, tokens_dev)
    first = lax.broadcasted_iota(jnp.int32, square, 0)
    second = lax.broadcasted_iota(jnp.int32, square, 1)

    def ones_where(mask):
        return jnp.where(mask, 1.0, 0.0).astype(jnp.bfloat16)

    chosen = jnp.where(jnp.broadcast_to(row_ref[...], square) == first, 1.0, 0.0)
    to_cells = chosen.astype(jnp.bfloat16)
    to_slots = chosen.T.astype(jnp.bfloat16)
    same = ones_where(first == second)
    spot = first % CROSS
    shifts = (
        ones_where((second == first - 1) & (spot > 0)),
        ones_where((second == first + 1) & (spot < CROSS - 1)),
    )

    def times(left, right):
        return jnp.dot(left, right, preferred_element_type=jnp.float32)

    def clear(field):
        pad = jnp.zeros((CROSS, width), jnp.float32)
        for shift in range(3):
            for z in range(depth + 2):
                field[shift, z, 0] = pad
                field[shift, z, INLINE + 1] = pad

    def fill(field, layers, value):
        versions = (times(shifts[0], value), value.astype(jnp.float32), times(shifts[1], value))
        for shift in range(3):
            for at, z in enumerate(layers):
                field[shift, z, pl.ds(1, INLINE)] = versions[shift][
                    at * layer : (at + 1) * layer
                ].reshape(INLINE, CROSS, width)

    def halo_pair(which):
        up = remote(
            edge.at[which, 0],
            halo.at[which, 1],
            halo_s.at[which, 0],
            halo_r.at[which, 0],
            {"seq": (me + count - 1) % count},
        )
        down = remote(
            edge.at[which, 1],
            halo.at[which, 0],
            halo_s.at[which, 1],
            halo_r.at[which, 1],
            {"seq": (me + 1) % count},
        )
        return (up, down)

    def halo_start(which, value):
        edge[which, 0] = value[:layer]
        edge[which, 1] = value[tokens_dev - layer :]
        up, down = halo_pair(which)

        @pl.when(me > 0)
        def _():
            up.start()

        @pl.when(me < count - 1)
        def _():
            down.start()

    def halo_finish(which, field):
        up, down = halo_pair(which)

        @pl.when(me > 0)
        def _():
            down.wait_recv()
            up.wait_send()

        @pl.when(me < count - 1)
        def _():
            up.wait_recv()
            down.wait_send()

        fill(field, (0, depth + 1), halo[which].reshape(2 * layer, width))

    def window(field, z, i, c, lanes):
        return field[c, pl.ds(z, depth), pl.ds(i, INLINE), :, lanes]

    def lanes_of(j):
        return pl.ds(pl.multiple_of(j * LANES, LANES), LANES)

    def convolve(field, flip, start, stop):
        def body(j, carry):
            lanes = lanes_of(j)
            result = window(field, 1, 1, 1, lanes)
            for offset in range(27):
                z, i, c = (offset // 9, offset // 3 % 3, offset % 3)
                if flip:
                    z, i, c = (2 - z, 2 - i, 2 - c)
                result = result + ker_ref[pl.ds(offset, 1), lanes] * window(field, z, i, c, lanes)
            cells[:, lanes] = result.reshape(tokens_dev, LANES).astype(jnp.bfloat16)
            return carry

        lax.fori_loop(start, stop, body, 0)

    def kernel_sums():
        def body(j, carry):
            lanes = lanes_of(j)
            grad = window(field_d, 1, 1, 1, lanes)
            for offset in range(27):
                z, i, c = (offset // 9, offset // 3 % 3, offset % 3)
                product = grad * window(field_x, z, i, c, lanes)
                sums[pl.ds(offset, 1), lanes] = jnp.sum(
                    product.reshape(tokens_dev, LANES), axis=0, keepdims=True
                )
            return carry

        lax.fori_loop(0, width // LANES, body, 0)

    tile = 2 * LANES
    chunks = width // LANES
    own_layers = tuple(range(1, depth + 1))

    def turn_body(n, carry):
        at = pl.multiple_of(n * LANES, LANES)
        turned[pl.ds(at, LANES), :] = (
            dp_ref[:, pl.ds(at, LANES)].astype(jnp.float32).T.astype(jnp.bfloat16)
        )
        return carry

    def back_chip(position):
        at = pl.ds(pl.multiple_of(at_ring(position) // 2 * (2 * rows), 16), 2 * rows)
        back_rows[at, :] = times(w_all[at, :], turned[...]).astype(jnp.bfloat16)

    def back_step(hop):
        for way in range(2):
            for copy in to_sibling.get((way, hop), ()):
                copy.wait_recv()
        if hop <= min(hops):
            back_chip(ring - hop)
        if hop > 0:
            back_chip(ring + hop)

    lax.fori_loop(0, w_ref.shape[1] // LANES, turn_body, 0)
    clear(field_x)
    clear(field_d)
    ring_step(1)
    move_x = exchange(0, tok_ref)
    back_step(0)
    ring_step(2)
    across_step(1)
    grid_x = times(to_cells, landed(0, move_x)).astype(jnp.bfloat16)
    halo_start(0, grid_x)
    fill(field_x, own_layers, grid_x)
    for hop in range(3, line + 1):
        ring_step(hop)
        across_step(hop - 1)
        back_step(hop - 2)
        if hop == line - 1:
            halo_finish(0, field_x)
            convolve(field_x, False, 0, chunks)
            move_y = outgoing(1, times(to_slots, cells[...]))
    back_step(line - 1)
    across_step(line)
    back_step(line)

    move_d = outgoing(
        2,
        lax.dot_general(
            same,
            back_rows[...],
            (((1,), (1,)), ((), ())),
            preferred_element_type=jnp.float32,
        ),
    )
    rows_y = landed(1, move_y)
    tiles = w_ref.shape[1] // tile

    def front_body(n, carry):
        at = pl.multiple_of(n * tile, tile)
        proj_ref[:, pl.ds(at, tile)] = times(rows_y, w_all[:, pl.ds(at, tile)]).astype(
            jnp.bfloat16
        )
        return carry

    lax.fori_loop(0, tiles // 2, front_body, 0)

    grid_d = times(to_cells, landed(2, move_d)).astype(jnp.bfloat16)
    halo_start(1, grid_d)
    fill(field_d, own_layers, grid_d)
    sums[pl.ds(3 * CROSS, CROSS)] = jnp.zeros((CROSS, width), jnp.float32)
    kernel_sums()

    def start_all(copies):
        for copy in copies:
            copy.start()
        sent.extend(copies)
        return copies

    def part_rows(core_at, plane_at):
        return pl.ds(pl.multiple_of((core_at * 2 + plane_at) * CROSS, CROSS), CROSS)

    home = part_rows(core, plane)
    squad = (
        (1 - core, plane, {"seq": sibling}),
        (core, 1 - plane, {"dp": 1 - plane}),
        (1 - core, 1 - plane, {"dp": 1 - plane, "seq": sibling}),
    )

    def scatter_sums():
        return start_all(
            [
                remote(
                    sums.at[part_rows(core_at, plane_at)],
                    arrived.at[k],
                    sum_s.at[0, k],
                    sum_r.at[0, k],
                    target,
                )
                for k, (core_at, plane_at, target) in enumerate(squad)
            ]
        )

    def pair_sums(copies):
        for copy in copies:
            copy.wait_recv()
        paired[...] = sums[home] + arrived[0] + arrived[1] + arrived[2]
        target = {"seq": me + 2 - 4 * chip_y}
        return start_all([remote(paired, arrived.at[3], sum_s.at[1, 0], sum_r.at[1, 0], target)])

    def line_sums(copies):
        for copy in copies:
            copy.wait_recv()
        layers[chip_z] = paired[...] + arrived[3]
        return start_all(
            [
                remote(
                    layers.at[chip_z],
                    layers.at[chip_z],
                    sum_s.at[2, k],
                    sum_r.at[2, k],
                    {"seq": (chip_z + k) % line * 4 + chip_y * 2 + core},
                )
                for k in range(1, line)
            ]
        )

    def share_sums(copies):
        for copy in copies:
            copy.wait_recv()
        whole_sum = layers[0]
        for k in range(1, line):
            whole_sum = whole_sum + layers[k]
        total[home] = whole_sum
        return start_all(
            [
                remote(total.at[home], total.at[home], sum_s.at[3, k], sum_r.at[3, k], target)
                for k, (core_at, plane_at, target) in enumerate(squad)
            ]
        )

    def finish_sums(copies):
        for copy in copies:
            copy.wait_recv()
        dker_ref[...] = total[: dker_ref.shape[0]]

    summing = scatter_sums()
    halo_finish(1, field_d)
    convolve(field_d, True, 0, chunks // 2)
    summing = pair_sums(summing)
    convolve(field_d, True, chunks // 2, chunks)
    summing = line_sums(summing)
    move_b = outgoing(3, times(to_slots, cells[...]))

    lax.fori_loop(tiles // 2, tiles * 3 // 4, front_body, 0)
    summing = share_sums(summing)
    lax.fori_loop(tiles * 3 // 4, tiles, front_body, 0)
    finish_sums(summing)
    dtok_ref[...] = landed(3, move_b)
    for copy in sent:
        copy.wait_send()


def copy_results(proj_in, dtok_in, dker_in, proj_out, dtok_out, dker_out):
    proj_out[...] = proj_in[...]
    dtok_out[...] = dtok_in[...]
    dker_out[...] = dker_in[...]


def fused_shards(tokens, place, kernel, proj_weight, d_projected):
    count = lax.axis_size("seq")
    tokens_dev, width = tokens.shape[1:]
    columns = proj_weight.shape[1]
    layer = INLINE * CROSS
    group = tokens_dev // count
    depth = tokens_dev // layer
    line = count // 4
    taps = kernel.shape[0]
    vmem = pl.BlockSpec(memory_space=pltpu.VMEM)
    dma = pltpu.SemaphoreType.DMA
    bf16, f32 = (jnp.bfloat16, jnp.float32)
    projected, d_tokens, d_kernel = pl.pallas_call(
        functools.partial(fused, count),
        out_shape=(
            jax.ShapeDtypeStruct((tokens_dev, columns), bf16),
            jax.ShapeDtypeStruct((tokens_dev, width), bf16),
            jax.ShapeDtypeStruct((taps, width), f32),
        ),
        in_specs=[vmem] * 5,
        out_specs=(vmem, vmem, vmem),
        scratch_shapes=[
            pltpu.VMEM((width, columns), bf16),
            pltpu.VMEM((4, count, group, width), bf16),
            pltpu.VMEM((4, count, group, width), bf16),
            pltpu.VMEM((2, 2, layer, width), bf16),
            pltpu.VMEM((2, 2, layer, width), bf16),
            pltpu.VMEM((3, depth + 2, INLINE + 2, CROSS, width), f32),
            pltpu.VMEM((3, depth + 2, INLINE + 2, CROSS, width), f32),
            pltpu.VMEM((tokens_dev, width), bf16),
            pltpu.VMEM((columns, tokens_dev), bf16),
            pltpu.VMEM((width, tokens_dev), bf16),
            pltpu.VMEM((4 * CROSS, width), f32),
            pltpu.VMEM((4, CROSS, width), f32),
            pltpu.VMEM((CROSS, width), f32),
            pltpu.VMEM((line, CROSS, width), f32),
            pltpu.VMEM((4 * CROSS, width), f32),
            dma((4, count)),
            dma((4, count)),
            dma((2, line + 1, 4)),
            dma((2, line + 1, 4)),
            dma((2, line + 1, 2)),
            dma((2, line + 1, 2)),
            dma((3, line + 1, 6)),
            dma((3, line + 1, 6)),
            dma((2, 2)),
            dma((2, 2)),
            dma((4, 4)),
            dma((4, 4)),
        ],
        compiler_params=pltpu.CompilerParams(
            collective_id=0, has_side_effects=True, vmem_limit_bytes=56 * 1024 * 1024
        ),
        cost_estimate=pl.CostEstimate(
            flops=4 * tokens_dev * width * columns,
            bytes_accessed=4 * tokens_dev * columns,
            transcendentals=0,
        ),
    )(
        tokens[0].reshape(count, group, width),
        place,
        kernel,
        proj_weight,
        d_projected[0],
    )
    results = [projected, d_tokens, d_kernel]
    projected, d_tokens, d_kernel = pl.pallas_call(
        copy_results,
        out_shape=tuple(jax.ShapeDtypeStruct(r.shape, r.dtype) for r in results),
        in_specs=[vmem] * 3,
        out_specs=(vmem,) * 3,
    )(*results)
    return (projected[None], d_tokens[None], d_kernel)


def solution(mesh):
    placed = (P("dp", "seq", None), P("seq", None), P(), P("seq", None), P("dp", "seq", None))
    count = mesh.shape["seq"]
    use_kernel = mesh.shape["dp"] == 2 and count == 16
    return jax.shard_map(
        fused_shards if use_kernel else shards,
        mesh=mesh,
        in_specs=placed,
        out_specs=(P("dp", "seq", None), P("dp", "seq", None), P()),
        check_vma=False,
    )
```
